32 devices in a mesh: groups: 2 (over x), gx: 16 (over z, y, core).
Axes of the slice: x: 2, y: 2, z: 4, core: 2. Of those that a mesh axis runs over, the one named last changes fastest.
Arguments:
- adjoint_state: float32 [8, 96, 128, 128], P(None, 'groups', 'gx'), parts along dimension 1, may hold values from -6 to 6
- forward_fields: bfloat16 [2, 3, 96, 128, 128], P(None, None, 'groups', 'gx'), parts along dimension 2, may hold values from -6 to 6
- vel_coeffs: float32 [8, 128], P('groups'), parts along dimension 0, may hold values from 0.2 to 0.8
- stress_coeffs: float32 [8, 128], P('groups'), parts along dimension 0, may hold values from 0.15 to 0.6
- drm_cells: int32 [4096], P('gx'), may hold values from 120 to 16383, as said below
- drm_force: float32 [32, 2, 2, 4096], P('groups', None, None, 'gx'), parts along dimension 0, may hold values from -6 to 6
- source_id: int32 [96], P('groups'), parts along dimension 0, may hold values from 0 to 15
Outputs:
- adjoint_out: float32 [8, 96, 128, 128], P(None, 'groups', 'gx'), parts along dimension 1
- gradients: float32 [4, 128], P('groups'), parts along dimension 0
The draws below stay inside these ranges and needn't reach their ends.
There are 2 independent parts, one for each index of `groups`. The reference program is written for one: setup_inputs(seed, part) draws one part's arguments, and reference() takes and returns one part's arrays. A program takes and returns all parts, laid end to end along the dimension named above; an argument that names none is the same for every part. Nothing has to cross between parts.
Inputs may be any that keep to these rules, and one draw needn't show every extreme that they name: `drm_cells`: in each aligned block b of 256 entries, every entry names a cell x * 128 + z with b * 8 <= x < (b + 1) * 8 and 120 <= z < 128; cells may repeat.
All inputs are finite; a program needn't handle non-finite values.
Results may differ from the reference program's by a relative error of at most 0.0003.
Values sent between devices are 32-bit elements; how exact they have to be, the bound alone decides.
A program may use at most 64 MiB of HBM per device.

```python
import math
import jax
import jax.numpy as jnp

CX = 8
NZ = 128
EVENTS = 48
NSRC = 16
STEPS = 2
LAYER = 8
DRM_DEV = 256
NX = 128
NDRM = 4096


def draw_drm_cells(key, part):
    block_count = NDRM // DRM_DEV
    key_lateral, key_depth = jax.random.split(key)
    lateral = jax.random.randint(key_lateral, (block_count, DRM_DEV), 0, CX)
    depth_index = jax.random.randint(key_depth, (block_count, DRM_DEV), NZ - LAYER, NZ)
    lateral = lateral.at[:, 0].set(0).at[:, DRM_DEV - 1].set(CX - 1)
    depth_index = depth_index.at[:, 0].set(NZ - LAYER).at[:, DRM_DEV - 1].set(NZ - 1)
    offsets = (jnp.arange(block_count, dtype=jnp.int32) * CX)[:, None]
    return ((lateral + offsets) * NZ + depth_index).reshape(-1).astype(jnp.int32)


def plant(entries, rng, least, high):
    longest = entries.shape.index(max(entries.shape))
    spots = []
    for shift in (0, 1):
        where = [jax.random.randint(jax.random.fold_in(rng, axis), (), 0, length) for axis, length in enumerate(entries.shape)]
        where[longest] = (where[longest] + shift) % entries.shape[longest]
        spots.append(tuple(where))
    return entries.at[spots[0]].set(least).at[spots[1]].set(high)


def block_scale(stream_key, extent, shards, least, high):
    gain, own = 1.0, jax.random.fold_in(stream_key, 6)
    for axis_at, shards_of in shards:
        steps = jnp.exp(jax.random.uniform(jax.random.fold_in(own, axis_at), (shards_of,), jnp.float32, least / len(shards), high / len(shards)))
        gain = gain * jnp.repeat(steps, extent[axis_at] // shards_of).reshape([-1 if axis == axis_at else 1 for axis in range(len(extent))])
    return gain


def noise(own_key, shape, width, bound, pieces=(), held_as=jnp.bfloat16):
    factor_of = block_scale(own_key, shape, pieces, -0.22, 0.18) if pieces else 1.0
    result = jax.random.normal(own_key, shape, jnp.float32) * width * factor_of
    return jnp.minimum(jnp.maximum(result, -bound), bound).astype(held_as)


def setup_inputs(seed: int = 0, part: int = 0) -> dict:
    streams_of = jax.random.split(jax.random.key(seed), 8)
    part_splits = jax.random.split(jax.random.fold_in(streams_of[7], part), 8)
    return {
        "adjoint_state": noise(part_splits[0], (8, EVENTS, NX, NZ), 1.0, 6.0, ((2, 16),), jnp.float32),
        "forward_fields": noise(part_splits[1], (STEPS, 3, EVENTS, NX, NZ), 1.0, 6.0, ((3, 16),)),
        "vel_coeffs": jnp.clip(jnp.exp(jax.random.uniform(part_splits[2], (4, NZ), jnp.float32, math.log(0.2), math.log(0.8))), 0.2, 0.8),
        "stress_coeffs": jnp.clip(jnp.exp(jax.random.uniform(part_splits[3], (4, NZ), jnp.float32, math.log(0.15), math.log(0.6))), 0.15, 0.6),
        "drm_cells": draw_drm_cells(jax.random.fold_in(streams_of[7], 71), part),
        "drm_force": noise(part_splits[5], (NSRC, STEPS, 2, NDRM), 1.0, 6.0, ((3, 16),), jnp.float32),
        "source_id": plant(jax.random.randint(part_splits[6], (EVENTS,), 0, NSRC), jax.random.fold_in(part_splits[6], 1), 0, NSRC - 1).astype(jnp.int32),
    }


def lower_diff(values, before):
    return values - jnp.concatenate([before, values[:, :-1]], axis=1)


def upper_diff(values, beyond):
    return jnp.concatenate([values[:, 1:], beyond], axis=1) - values


def depth_lower(values):
    return values - jnp.concatenate([jnp.zeros_like(values[:, :, :1]), values[:, :, :-1]], axis=2)


def depth_upper(values):
    return jnp.concatenate([values[:, :, 1:], jnp.zeros_like(values[:, :, :1])], axis=2) - values


def velocity_update(fields, before, forcing, vel_coeffs):
    vel_x, vel_z, flow_x, flow_z, stress_xx, stress_zz, stress_xz, pressure = fields
    mass_solid, mass_couple, mass_fluid, drag_rate = vel_coeffs[0], vel_coeffs[1], vel_coeffs[2], vel_coeffs[3]
    force_x = lower_diff(stress_xx, before[0]) + depth_lower(stress_xz)
    force_z = lower_diff(stress_xz, before[1]) + depth_lower(stress_zz)
    push_x = lower_diff(pressure, before[2]) + drag_rate * flow_x
    push_z = depth_lower(pressure) + drag_rate * flow_z
    vel_x = vel_x + mass_solid * force_x + mass_couple * push_x + forcing[0]
    vel_z = vel_z + mass_solid * force_z + mass_couple * push_z + forcing[1]
    flow_x = flow_x - mass_couple * force_x - mass_fluid * push_x
    flow_z = flow_z - mass_couple * force_z - mass_fluid * push_z
    return [vel_x, vel_z, flow_x, flow_z, stress_xx, stress_zz, stress_xz, pressure]


def stress_update(fields, beyond, stress_coeffs):
    vel_x, vel_z, flow_x, flow_z, stress_xx, stress_zz, stress_xz, pressure = fields
    lame_total, shear_modulus, coupling, fluid_modulus = stress_coeffs[0], stress_coeffs[1], stress_coeffs[2], stress_coeffs[3]
    strain_x = upper_diff(vel_x, beyond[0])
    strain_z = depth_upper(vel_z)
    dilation = strain_x + strain_z
    inflow = upper_diff(flow_x, beyond[2]) + depth_upper(flow_z)
    stress_xx = stress_xx + lame_total * dilation + 2.0 * shear_modulus * strain_x - coupling * inflow
    stress_zz = stress_zz + lame_total * dilation + 2.0 * shear_modulus * strain_z - coupling * inflow
    stress_xz = stress_xz + shear_modulus * (depth_upper(vel_x) + upper_diff(vel_z, beyond[1]))
    pressure = pressure - coupling * dilation - fluid_modulus * inflow
    return [vel_x, vel_z, flow_x, flow_z, stress_xx, stress_zz, stress_xz, pressure]


def reference(adjoint_state, forward_fields, vel_coeffs, stress_coeffs, drm_cells, drm_force, source_id):
    fields = [adjoint_state[field_index] for field_index in range(8)]
    zero_rim = jnp.zeros((EVENTS, 1, NZ), jnp.float32)
    rims = [zero_rim, zero_rim, zero_rim]
    selected = drm_force[source_id]
    perm_total = jnp.zeros((NZ,), jnp.float32)
    poro_total = jnp.zeros((NZ,), jnp.float32)
    for step_index in range(STEPS):
        drm_term = jnp.transpose(selected[:, step_index], (1, 0, 2))
        forcing_plane = jnp.zeros((2, EVENTS, NX * NZ), jnp.float32).at[:, :, drm_cells].add(drm_term)
        forcing_plane = forcing_plane.reshape(2, EVENTS, NX, NZ)
        fields = velocity_update(fields, rims, forcing_plane, vel_coeffs)
        flow_prod = fields[2] * forward_fields[step_index, 0].astype(jnp.float32) + fields[3] * forward_fields[step_index, 1].astype(jnp.float32)
        perm_total = perm_total + jnp.sum(flow_prod, axis=(0, 1))
        fields = stress_update(fields, rims, stress_coeffs)
        poro_total = poro_total + jnp.sum(fields[7] * forward_fields[step_index, 2].astype(jnp.float32), axis=(0, 1))
    normalizer = (EVENTS * NX) ** -0.5
    gradients = jnp.stack([vel_coeffs[2] * vel_coeffs[3] * perm_total, stress_coeffs[3] * poro_total]) * normalizer
    return jnp.stack(fields), gradients
```

```python
import functools

import jax
import jax.numpy as jnp
from jax import lax
from jax.experimental import pallas as pl
from jax.experimental.pallas import tpu as pltpu
from jax.sharding import PartitionSpec as P

CHUNKS = 2
VX, VZ, QX, QZ, XX, ZZ, XZ, PR = range(8)


def coeff_rows(coeffs):
    return [coeffs[i : i + 1] for i in range(4)]


def depth_lower(values, lane):
    return values - jnp.where(lane == 0, 0.0, pltpu.roll(values, 1, 1))


def depth_upper(values, lane):
    last = values.shape[1] - 1
    return jnp.where(lane == last, 0.0, pltpu.roll(values, last, 1)) - values


def velocity(fields, sides, vel, lane, forcing=None):
    vel_x, vel_z, flow_x, flow_z, _, stress_zz, stress_xz, pressure = fields
    solid, couple, fluid, drag = vel
    force_x = sides[0] + depth_lower(stress_xz, lane)
    force_z = sides[1] + depth_lower(stress_zz, lane)
    push_x = sides[2] + drag * flow_x
    push_z = depth_lower(pressure, lane) + drag * flow_z
    new_x = vel_x + solid * force_x + couple * push_x
    new_z = vel_z + solid * force_z + couple * push_z
    if forcing is not None:
        new_x = new_x + forcing[0]
        new_z = new_z + forcing[1]
    flow_x = flow_x - couple * force_x - fluid * push_x
    flow_z = flow_z - couple * force_z - fluid * push_z
    return [new_x, new_z, flow_x, flow_z, *fields[4:]]


def stress(fields, sides, coeffs, lane):
    vel_x, vel_z, flow_x, flow_z, xx, zz, xz, pressure = fields
    lame, shear, couple, fluid = coeffs
    strain_z = depth_upper(vel_z, lane)
    dilation = sides[0] + strain_z
    inflow = sides[2] + depth_upper(flow_z, lane)
    shared = lame * dilation - couple * inflow
    twice = 2.0 * shear
    xx = xx + shared + twice * sides[0]
    zz = zz + shared + twice * strain_z
    xz = xz + shear * (depth_upper(vel_x, lane) + sides[1])
    pressure = pressure - couple * dilation - fluid * inflow
    return [vel_x, vel_z, flow_x, flow_z, xx, zz, xz, pressure]


def side_share(row, coeffs):
    lame, shear, couple, fluid = coeffs
    zz = lame * row[0] - couple * row[2]
    pressure = -couple * row[0] - fluid * row[2]
    return [zz + 2.0 * shear * row[0], zz, shear * row[1], pressure]


def beyond_share(row, coeffs):
    xx, _, xz, pressure = side_share(row, coeffs)
    return [xx, xz, pressure]


def edge(fields):
    return [fields[XX], fields[XZ], fields[PR]]


def front(fields):
    return [fields[VX], fields[VZ], fields[QX]]


def minus(first, second):
    return [a - b for a, b in zip(first, second)]


def plus(first, second):
    return [a + b for a, b in zip(first, second)]


def kernel(
    n, scale, st_hbm, fw_hbm, vc_hbm, sc_hbm, cell_hbm, df_hbm, sid_hbm, out_ref, grad_ref,
    st, fw, vc_ref, sc_ref, cell_ref, df_ref, sid_ref, flat, tab, wide, keep, up, down, low, high, sums,
    st_sem, fw_sem, small_sem, up_sem, down_sem, sum_send, sum_recv, here,
):
    _, cells, depth = st.shape
    events = up.shape[1]
    rows = cells // events
    sources = df_ref.shape[0]
    me = lax.axis_index("gx")
    part = cells // CHUNKS
    smalls = [
        pltpu.make_async_copy(src, dst, small_sem.at[i])
        for i, (src, dst) in enumerate(
            [(df_hbm, df_ref), (cell_hbm, cell_ref), (sid_hbm, sid_ref), (vc_hbm, vc_ref), (sc_hbm, sc_ref)]
        )
    ]
    for small in smalls:
        small.start()
    loads = []
    for c in range(CHUNKS):
        at = pl.ds(c * part, part)
        loads.append(pltpu.make_async_copy(st_hbm.at[:, at], st.at[:, at], st_sem.at[c]))
        loads[-1].start()
    fw_load = pltpu.make_async_copy(fw_hbm, fw, fw_sem)
    fw_load.start()

    barrier = pltpu.get_barrier_semaphore()

    def greet(semaphore, peer):
        pl.semaphore_signal(semaphore, inc=1, device_id={"gx": peer}, device_id_type=pl.DeviceIdType.MESH)

    @pl.when(me > 0)
    def _():
        greet(barrier, me - 1)

    lax.fori_loop(me + 1, n, lambda peer, _: greet(barrier, peer), None)

    for small in smalls:
        small.wait()
    vel = coeff_rows(vc_ref[...])
    coeffs = coeff_rows(sc_ref[...])

    force = jnp.concatenate([df_ref[:, t, c, :] for t in range(2) for c in range(2)], axis=0)
    first = force.astype(jnp.bfloat16)
    rest = force - first.astype(jnp.float32)
    second = rest.astype(jnp.bfloat16)
    third = (rest - second.astype(jnp.float32)).astype(jnp.bfloat16)
    pieces = jnp.concatenate([first, second, third], axis=0)
    count = force.shape[0]
    place = cell_ref[...] - me * (rows * depth)
    spot = lax.broadcasted_iota(jnp.int32, (depth, place.shape[1]), 0)
    planes = {}
    for x in range(rows):
        hot = jnp.where(spot + x * depth == place, 1.0, 0.0).astype(jnp.bfloat16)
        got = lax.dot_general(pieces, hot, (((1,), (1,)), ((), ())), preferred_element_type=jnp.float32)
        got = got[:count] + got[count : 2 * count] + got[2 * count :]
        flat[pl.ds(x, count, stride=rows), :] = got
        planes[x] = got
    tab[...] = flat[...].reshape(tab.shape)

    row_id = lax.broadcasted_iota(jnp.int32, (8, sources), 0)
    source_at = lax.broadcasted_iota(jnp.int32, (8, sources), 1)
    blocks = []
    for b in range(events // 8):
        wanted = jnp.full((8, sources), sid_ref[b * 8], jnp.int32)
        for r in range(1, 8):
            wanted = jnp.where(row_id == r, sid_ref[b * 8 + r], wanted)
        blocks.append(jnp.where(wanted == source_at, 1.0, 0.0))
    picked = jnp.concatenate(blocks, axis=0)

    def row_forcing(x, t):
        return [
            jnp.dot(
                picked, planes[x][(t * 2 + c) * sources : (t * 2 + c + 1) * sources],
                precision=lax.Precision.HIGHEST, preferred_element_type=jnp.float32,
            )
            for c in range(2)
        ]

    last = rows - 1
    slot_of = {0: 0, 1: 8, last: 16, last - 1: 24}
    force_0, force_1, force_last = row_forcing(0, 0), row_forcing(1, 0), row_forcing(last, 0)
    later_0 = row_forcing(0, 1)

    lane = lax.broadcasted_iota(jnp.int32, (8, depth), 1)
    at_row = lax.broadcasted_iota(jnp.int32, (rows, depth), 0)
    zero = jnp.zeros((8, depth), jnp.float32)
    blocks = range(events // 8)

    per_chunk = events // 8 // CHUNKS
    ups, downs = [], []
    for c in range(CHUNKS):
        some = pl.ds(c * per_chunk * 8, per_chunk * 8)
        ups.append(
            pltpu.make_async_remote_copy(
                up.at[:, some], low.at[:, some], up_sem.at[0, c], up_sem.at[1, c],
                device_id={"gx": jnp.minimum(me + 1, n - 1)}, device_id_type=pl.DeviceIdType.MESH,
            )
        )
        downs.append(
            pltpu.make_async_remote_copy(
                down.at[:, some], high.at[:, some], down_sem.at[0, c], down_sem.at[1, c],
                device_id={"gx": jnp.maximum(me - 1, 0)}, device_id_type=pl.DeviceIdType.MESH,
            )
        )

    for b in blocks:
        mine = slice(b * 8, (b + 1) * 8)
        c = b // per_chunk
        if b % per_chunk == 0:
            loads[c].wait()

        def row(x, names=range(8)):
            return [st[f, pl.ds(b * 8 * rows + x, 8, stride=rows), :] for f in names]

        row_last = row(last)
        sides = minus(edge(row_last), row(last - 1, (XX, XZ, PR)))
        one_last = velocity(row_last, sides, vel, lane, [v[mine] for v in force_last])
        one_last = stress(one_last, [-v for v in front(one_last)], coeffs, lane)
        for i, v in enumerate(edge(row_last) + edge(one_last)):
            up[i, mine, :] = v
        row_0, row_1 = row(0), row(1)
        one_0 = velocity(row_0, edge(row_0), vel, lane, [v[mine] for v in force_0])
        sides = minus(edge(row_1), edge(row_0))
        one_1 = velocity(row_1, sides, vel, lane, [v[mine] for v in force_1])
        two_0 = stress(one_0, minus(front(one_1), front(one_0)), coeffs, lane)
        two_0 = velocity(two_0, edge(two_0), vel, lane, [v[mine] for v in later_0])
        for i, v in enumerate(front(one_0) + front(two_0)):
            down[i, mine, :] = v
        if b % per_chunk == per_chunk - 1:
            if c == 0:
                pl.semaphore_wait(barrier, me + jnp.where(me < n - 1, 1, 0))
            pl.when(me < n - 1)(ups[c].start)
            pl.when(me > 0)(downs[c].start)

    lax.fori_loop(0, me, lambda peer, _: greet(here, peer), None)
    fw_load.wait()

    def lower(values):
        return values - jnp.where(at_row == 0, 0.0, pltpu.roll(values, 1, 0))

    def upper(values):
        return jnp.where(at_row == last, 0.0, pltpu.roll(values, last, 0)) - values

    def pair(i, totals):
        perm, poro = totals
        both = pl.ds(pl.multiple_of(i * 2 * rows, 2 * rows), 2 * rows)
        stored = [fw[k, both, :].astype(jnp.float32) for k in range(6)]
        for k in range(6):
            wide[k, both, :] = stored[k]
        for half in range(2):
            e = i * 2 + half
            at = pl.ds(pl.multiple_of(e * rows, rows), rows)
            own = slice(half * rows, (half + 1) * rows)
            source = sid_ref[e]
            fields = [st[f, at, :] for f in range(8)]
            for t in range(2):
                forcing = [tab[(t * 2 + c) * sources + source] for c in range(2)]
                fields = velocity(fields, [lower(v) for v in edge(fields)], vel, lane, forcing)
                perm = perm + fields[QX] * stored[3 * t][own] + fields[QZ] * stored[3 * t + 1][own]
                fields = stress(fields, [upper(v) for v in front(fields)], coeffs, lane)
                poro = poro + fields[PR] * stored[3 * t + 2][own]
            for f in range(8):
                out_ref[f, at, :] = fields[f]
        return perm, poro

    perm, poro = lax.fori_loop(0, events // 2, pair, (zero, zero), unroll=4)

    @pl.when(me == 0)
    def _():
        low[...] = jnp.zeros(low.shape, jnp.float32)

    @pl.when(me == n - 1)
    def _():
        high[...] = jnp.zeros(high.shape, jnp.float32)

    has_low = jnp.where(me > 0, 1.0, 0.0)
    has_high = jnp.where(me < n - 1, 1.0, 0.0)

    for b in blocks:
        mine = slice(b * 8, (b + 1) * 8)
        if b % per_chunk == 0:
            pl.when(me > 0)(ups[b // per_chunk].wait_recv)
            pl.when(me < n - 1)(downs[b // per_chunk].wait_recv)

        def seen(k, x):
            return wide[k, pl.ds(b * 8 * rows + x, 8, stride=rows), :]

        def add(x, names, values):
            for f, v in zip(names, values):
                keep[slot_of[x] + f, mine, :] = v

        one = velocity([zero] * 8, [-low[i, mine, :] for i in range(3)], vel, lane)
        perm = perm + one[QX] * seen(0, 0) + one[QZ] * seen(1, 0)
        met = plus([down[i, mine, :] for i in range(3)], front(one))
        rim = [low[3 + i, mine, :] + v for i, v in enumerate(beyond_share(met, coeffs))]
        rim = [v * has_low for v in rim]
        two = stress(one, [-v for v in front(one)], coeffs, lane)
        poro = poro + two[PR] * seen(2, 0)
        next_two = velocity([zero] * 8, [-v for v in edge(two)], vel, lane)
        two = velocity(two, minus(edge(two), rim), vel, lane)
        perm = perm + two[QX] * seen(3, 0) + two[QZ] * seen(4, 0)
        perm = perm + next_two[QX] * seen(3, 1) + next_two[QZ] * seen(4, 1)
        two = stress(two, minus(front(next_two), front(two)), coeffs, lane)
        next_two = stress(next_two, [-v for v in front(next_two)], coeffs, lane)
        poro = poro + two[PR] * seen(5, 0) + next_two[PR] * seen(5, 1)
        add(0, range(8), two)
        add(1, range(8), next_two)

        edge_last = [up[i, mine, :] for i in range(3)]
        one = velocity([zero] * 8, [-v for v in edge_last], vel, lane)
        met = [(high[i, mine, :] + v) * has_high for i, v in enumerate(front(one))]
        own = [zero] * 4 + side_share(met, coeffs)
        poro = poro + own[PR] * seen(2, last)
        two = stress(one, [-v for v in front(one)], coeffs, lane)
        full = [up[3 + i, mine, :] + v for i, v in enumerate(edge(own))]
        two = velocity(two, minus(edge(two), full), vel, lane)
        met = [(high[3 + i, mine, :] + v) * has_high for i, v in enumerate(front(two))]
        own = velocity(own, edge(own), vel, lane)
        perm = perm + own[QX] * seen(3, last) + own[QZ] * seen(4, last)
        prior = side_share(front(own), coeffs)
        own = stress(own, minus(met, front(own)), coeffs, lane)
        poro = poro + own[PR] * seen(5, last) + prior[3] * seen(5, last - 1)
        add(last, range(8), own)
        add(last - 1, range(XX, 8), prior)

    totals = (perm, poro)
    sums[me] = jnp.concatenate([jnp.sum(total, axis=0, keepdims=True) for total in totals], axis=0)

    @pl.when(me < n - 1)
    def _():
        pl.semaphore_wait(here, n - 1 - me)

    def send(peer, _):
        @pl.when(peer != me)
        def _():
            pltpu.make_async_remote_copy(
                sums.at[me], sums.at[me], sum_send, sum_recv,
                device_id={"gx": peer}, device_id_type=pl.DeviceIdType.MESH,
            ).start()

    lax.fori_loop(0, n, send, None)
    for b in blocks:
        for x in (0, 1, last, last - 1):
            at = pl.ds(b * 8 * rows + x, 8, stride=rows)
            for f in range(XX if x == last - 1 else 0, 8):
                out_ref[f, at, :] = out_ref[f, at, :] + keep[slot_of[x] + f, b * 8 : (b + 1) * 8, :]
    pltpu.make_async_copy(sums.at[pl.ds(1, n - 1)], sums.at[pl.ds(0, n - 1)], sum_recv).wait()
    mine = jnp.sum(sums[...], axis=0)
    grad_ref[0:1, :] = vel[2] * vel[3] * mine[0:1] * scale
    grad_ref[1:2, :] = coeffs[3] * mine[1:2] * scale
    pltpu.make_async_copy(sums.at[pl.ds(1, n - 1)], sums.at[pl.ds(0, n - 1)], sum_send).wait()
    for c in range(CHUNKS):
        pl.when(me < n - 1)(ups[c].wait_send)
        pl.when(me > 0)(downs[c].wait_send)


def write(out_ref, grad_ref, out_hbm, grad_hbm, sems):
    fields = out_ref.shape[0]
    copies = [pltpu.make_async_copy(out_ref.at[f], out_hbm.at[f], sems.at[f]) for f in range(fields)]
    copies.append(pltpu.make_async_copy(grad_ref, grad_hbm, sems.at[fields]))
    for copy in copies:
        copy.start()
    for copy in copies:
        copy.wait()


def shards(adjoint_state, forward_fields, vel_coeffs, stress_coeffs, drm_cells, drm_force, source_id):
    fields, events, rows, depth = adjoint_state.shape
    cells = events * rows
    n = lax.axis_size("gx")
    scale = (events * rows * n) ** (-0.5)
    hbm, vmem = pl.BlockSpec(memory_space=pltpu.HBM), pl.BlockSpec(memory_space=pltpu.VMEM)
    f32 = jnp.float32
    dma = pltpu.SemaphoreType.DMA
    out, gradients = pl.pallas_call(
        functools.partial(kernel, n, scale),
        out_shape=[
            pltpu.VMEM((fields, cells, depth), f32),
            pltpu.VMEM((2, depth), f32),
        ],
        in_specs=[hbm] * 7,
        out_specs=[vmem, vmem],
        scratch_shapes=[
            pltpu.VMEM((fields, cells, depth), f32),
            pltpu.VMEM((6, cells, depth), jnp.bfloat16),
            pltpu.VMEM(vel_coeffs.shape, f32),
            pltpu.VMEM(stress_coeffs.shape, f32),
            pltpu.VMEM((1, drm_cells.shape[0]), jnp.int32),
            pltpu.VMEM(drm_force.shape, f32),
            pltpu.SMEM(source_id.shape, jnp.int32),
            pltpu.VMEM((4 * drm_force.shape[0] * rows, depth), f32),
            pltpu.VMEM((4 * drm_force.shape[0], rows, depth), f32),
            pltpu.VMEM((6, cells, depth), f32),
            pltpu.VMEM((32, events, depth), f32),
            pltpu.VMEM((6, events, depth), f32),
            pltpu.VMEM((6, events, depth), f32),
            pltpu.VMEM((6, events, depth), f32),
            pltpu.VMEM((6, events, depth), f32),
            pltpu.VMEM((n, 2, depth), f32),
            dma((CHUNKS,)),
            dma,
            dma((5,)),
            dma((2, CHUNKS)),
            dma((2, CHUNKS)),
            dma,
            dma,
            pltpu.SemaphoreType.REGULAR,
        ],
        compiler_params=pltpu.CompilerParams(
            collective_id=0, has_side_effects=True
        ),
    )(
        adjoint_state.reshape(fields, cells, depth),
        forward_fields.reshape(6, cells, depth),
        vel_coeffs,
        stress_coeffs,
        drm_cells.reshape(1, -1),
        drm_force,
        source_id,
    )
    out, gradients = pl.pallas_call(
        write,
        out_shape=[jax.ShapeDtypeStruct(out.shape, f32), jax.ShapeDtypeStruct(gradients.shape, f32)],
        in_specs=[pl.BlockSpec(memory_space=pl.ANY)] * 2,
        out_specs=[hbm, hbm],
        scratch_shapes=[dma((fields + 1,))],
    )(pltpu.with_memory_space_constraint(out, pltpu.VMEM), pltpu.with_memory_space_constraint(gradients, pltpu.VMEM))
    return out.reshape(adjoint_state.shape), gradients


def solution(mesh):
    in_specs = (
        P(None, "groups", "gx", None),
        P(None, None, "groups", "gx", None),
        P("groups", None),
        P("groups", None),
        P("gx"),
        P("groups", None, None, "gx"),
        P("groups"),
    )
    out_specs = (P(None, "groups", "gx", None), P("groups", None))
    return jax.shard_map(shards, mesh=mesh, in_specs=in_specs, out_specs=out_specs, check_vma=False)
```

```python
import functools

import jax
import jax.numpy as jnp
from jax import lax
from jax.experimental import pallas as pl
from jax.experimental.pallas import tpu as pltpu
from jax.sharding import PartitionSpec as P

LAYER = 8
VX, VZ, QX, QZ, XX, ZZ, XZ, PR = range(8)


def coeff_rows(coeffs):
    return [coeffs[i : i + 1] for i in range(4)]


def depth_lower(values, lane):
    return values - jnp.where(lane == 0, 0.0, pltpu.roll(values, 1, 1))


def depth_upper(values, lane):
    last = values.shape[1] - 1
    return jnp.where(lane == last, 0.0, pltpu.roll(values, last, 1)) - values


def velocity(fields, sides, vel, lane, forcing=None):
    vel_x, vel_z, flow_x, flow_z, _, stress_zz, stress_xz, pressure = fields
    solid, couple, fluid, drag = vel
    force_x = sides[0] + depth_lower(stress_xz, lane)
    force_z = sides[1] + depth_lower(stress_zz, lane)
    push_x = sides[2] + drag * flow_x
    push_z = depth_lower(pressure, lane) + drag * flow_z
    new_x = vel_x + solid * force_x + couple * push_x
    new_z = vel_z + solid * force_z + couple * push_z
    if forcing is not None:
        new_x = new_x + forcing[0]
        new_z = new_z + forcing[1]
    flow_x = flow_x - couple * force_x - fluid * push_x
    flow_z = flow_z - couple * force_z - fluid * push_z
    return [new_x, new_z, flow_x, flow_z, *fields[4:]]


def stress(fields, sides, coeffs, lane):
    vel_x, vel_z, flow_x, flow_z, xx, zz, xz, pressure = fields
    lame, shear, couple, fluid = coeffs
    strain_z = depth_upper(vel_z, lane)
    dilation = sides[0] + strain_z
    inflow = sides[2] + depth_upper(flow_z, lane)
    shared = lame * dilation - couple * inflow
    twice = 2.0 * shear
    xx = xx + shared + twice * sides[0]
    zz = zz + shared + twice * strain_z
    xz = xz + shear * (depth_upper(vel_x, lane) + sides[1])
    pressure = pressure - couple * dilation - fluid * inflow
    return [vel_x, vel_z, flow_x, flow_z, xx, zz, xz, pressure]


def side_share(row, coeffs):
    lame, shear, couple, fluid = coeffs
    zz = lame * row[0] - couple * row[2]
    pressure = -couple * row[0] - fluid * row[2]
    return [zz + 2.0 * shear * row[0], zz, shear * row[1], pressure]


def beyond_share(row, coeffs):
    xx, _, xz, pressure = side_share(row, coeffs)
    return [xx, xz, pressure]


def velocity_share(row, vel):
    solid, couple, fluid, _ = vel
    xx, xz, pressure = row
    return [-(solid * xx + couple * pressure), -solid * xz, couple * xx + fluid * pressure, couple * xz]


def stress_share(moved, sides, coeffs, lane):
    vel_x, vel_z, flow_x, flow_z = moved
    lame, shear, couple, fluid = coeffs
    strain_z = depth_upper(vel_z, lane)
    dilation = sides[0] + strain_z
    inflow = sides[2] + depth_upper(flow_z, lane)
    shared = lame * dilation - couple * inflow
    twice = 2.0 * shear
    return [
        shared + twice * sides[0],
        shared + twice * strain_z,
        shear * (depth_upper(vel_x, lane) + sides[1]),
        -couple * dilation - fluid * inflow,
    ]


def edge(fields):
    return [fields[XX], fields[XZ], fields[PR]]


def front(fields):
    return [fields[VX], fields[VZ], fields[QX]]


def minus(first, second):
    return [a - b for a, b in zip(first, second)]


def plus(first, second):
    return [a + b for a, b in zip(first, second)]


def kernel(
    n, scale, st_hbm, fw_hbm, vc_hbm, sc_hbm, cell_hbm, df_hbm, sid_hbm, out_ref, grad_ref,
    st, fw, vc_ref, sc_ref, cell_ref, df_ref, sid_ref, flat, tab, wide, keep, up, down, low, high, sums,
    st_sem, fw_sem, small_sem, up_sem, down_sem, sum_send, sum_recv, here,
):
    _, cells, depth = st.shape
    events = up.shape[1]
    rows = cells // events
    sources = df_ref.shape[0]
    me = lax.axis_index("gx")
    barrier = pltpu.get_barrier_semaphore()

    def greet(semaphore, peer):
        pl.semaphore_signal(semaphore, inc=1, device_id={"gx": peer}, device_id_type=pl.DeviceIdType.MESH)

    @pl.when(me > 0)
    def _():
        greet(barrier, me - 1)

    @pl.when(me < n - 1)
    def _():
        greet(barrier, me + 1)

    smalls = [
        pltpu.make_async_copy(src, dst, small_sem.at[i])
        for i, (src, dst) in enumerate(
            [(df_hbm, df_ref), (cell_hbm, cell_ref), (sid_hbm, sid_ref), (vc_hbm, vc_ref), (sc_hbm, sc_ref)]
        )
    ]
    for small in smalls:
        small.start()
    last = rows - 1
    from_hbm, to_vmem = st_hbm.reshape(8, events, rows, depth), st.reshape(8, events, rows, depth)
    loads = [
        pltpu.make_async_copy(from_hbm.at[:, :, at], to_vmem.at[:, :, at], st_sem.at[i])
        for i, at in enumerate([pl.ds(0, 2), pl.ds(last - 1, 2), pl.ds(2, rows - 4)])
    ]
    for load in loads:
        load.start()
    fw_load = pltpu.make_async_copy(fw_hbm, fw, fw_sem)
    fw_load.start()
    lax.fori_loop(me + 2, n, lambda peer, _: greet(barrier, peer), None)

    @pl.when(me == 0)
    def _():
        low[...] = jnp.zeros(low.shape, jnp.float32)

    @pl.when(me == n - 1)
    def _():
        high[...] = jnp.zeros(high.shape, jnp.float32)

    for small in smalls:
        small.wait()
    vel = coeff_rows(vc_ref[...])
    coeffs = coeff_rows(sc_ref[...])

    def three(values):
        first = values.astype(jnp.bfloat16)
        rest = values - first.astype(jnp.float32)
        second = rest.astype(jnp.bfloat16)
        return [first, second, (rest - second.astype(jnp.float32)).astype(jnp.bfloat16)]

    force = jnp.concatenate([df_ref[:, t, c, :] for t in range(2) for c in range(2)], axis=0)
    count = force.shape[0]
    place = cell_ref[...] - me * (rows * depth)
    column = lax.broadcasted_iota(jnp.int32, (depth, place.shape[1]), 0)
    spot = (column // LAYER) * depth + (depth - LAYER) + lax.rem(column, LAYER)
    hot = jnp.where(spot == place, 1.0, 0.0).astype(jnp.bfloat16)
    got = lax.dot_general(
        jnp.concatenate(three(force), axis=0), hot, (((1,), (1,)), ((), ())), preferred_element_type=jnp.float32
    )
    got = got[:count] + got[count : 2 * count] + got[2 * count :]

    def placed(values, x):
        at = lax.broadcasted_iota(jnp.int32, values.shape, 1)
        return jnp.where(at < depth - LAYER, 0.0, pltpu.roll(values, depth - LAYER - x * LAYER, 1))

    row_id = lax.broadcasted_iota(jnp.int32, (8, sources), 0)
    source_at = lax.broadcasted_iota(jnp.int32, (8, sources), 1)
    blocks = []
    for b in range(events // 8):
        wanted = jnp.full((8, sources), sid_ref[b * 8], jnp.int32)
        for r in range(1, 8):
            wanted = jnp.where(row_id == r, sid_ref[b * 8 + r], wanted)
        blocks.append(jnp.where(wanted == source_at, 1.0, 0.0))
    picked = jnp.concatenate(blocks, axis=0).astype(jnp.bfloat16)
    picked = jnp.concatenate([picked] * 3, axis=1)

    def event_forcing(t):
        return [
            jnp.dot(
                picked, jnp.concatenate(three(got[(t * 2 + c) * sources : (t * 2 + c + 1) * sources]), axis=0),
                preferred_element_type=jnp.float32,
            )
            for c in range(2)
        ]

    slot_of = {0: 0, 1: 8, last: 16, last - 1: 24}
    now, later = event_forcing(0), event_forcing(1)
    force_0, force_1, force_last = [[placed(v, x) for v in now] for x in (0, 1, last)]
    later_0 = [placed(v, 0) for v in later]

    lane = lax.broadcasted_iota(jnp.int32, (8, depth), 1)
    at_row = lax.broadcasted_iota(jnp.int32, (rows, depth), 0)
    zero = jnp.zeros((8, depth), jnp.float32)
    blocks = range(events // 8)

    ups, downs = [], []
    for c in range(2):
        half = pl.ds(3 * c, 3)
        ups.append(
            pltpu.make_async_remote_copy(
                up.at[half], low.at[half], up_sem.at[0, c], up_sem.at[1, c],
                device_id={"gx": jnp.minimum(me + 1, n - 1)}, device_id_type=pl.DeviceIdType.MESH,
            )
        )
    for c, part in enumerate([pl.ds(0, 3), pl.ds(3, 1), pl.ds(4, 2)]):
        downs.append(
            pltpu.make_async_remote_copy(
                down.at[part], high.at[part], down_sem.at[0, c], down_sem.at[1, c],
                device_id={"gx": jnp.maximum(me - 1, 0)}, device_id_type=pl.DeviceIdType.MESH,
            )
        )

    def own_block(b):
        return slice(b * 8, (b + 1) * 8)

    def row(b, x, names=range(8)):
        return [st[f, pl.ds(b * 8 * rows + x, 8, stride=rows), :] for f in names]

    loads[0].wait()
    firsts = []
    for b in blocks:
        row_0 = row(b, 0)
        one_0 = velocity(row_0, edge(row_0), vel, lane, [v[own_block(b)] for v in force_0])
        for i, v in enumerate(front(one_0)):
            down[i, own_block(b), :] = v
        firsts.append(one_0)
    pl.semaphore_wait(barrier, me + jnp.where(me < n - 1, 1, 0))
    pl.when(me > 0)(downs[0].start)
    loads[1].wait()
    for b in blocks:
        for i, v in enumerate(row(b, last, (XX, XZ, PR))):
            up[i, own_block(b), :] = v
    pl.when(me < n - 1)(ups[0].start)
    for b in blocks:
        mine = own_block(b)
        row_0, row_1, one_0 = row(b, 0, (XX, XZ, PR)), row(b, 1), firsts[b]
        one_1 = velocity(row_1, minus(edge(row_1), row_0), vel, lane, [v[mine] for v in force_1])
        two_0 = stress(one_0, minus(front(one_1), front(one_0)), coeffs, lane)
        two_0 = velocity(two_0, edge(two_0), vel, lane, [v[mine] for v in later_0])
        down[3, mine, :] = coeffs[2] * two_0[VX] + coeffs[3] * two_0[QX]
        down[4, mine, :] = two_0[VX]
        down[5, mine, :] = two_0[VZ]
    pl.when(me > 0)(downs[1].start)
    for b in blocks:
        mine = own_block(b)
        row_last = row(b, last)
        sides = minus(edge(row_last), row(b, last - 1, (XX, XZ, PR)))
        one_last = velocity(row_last, sides, vel, lane, [v[mine] for v in force_last])
        one_last = stress(one_last, [-v for v in front(one_last)], coeffs, lane)
        for i, v in enumerate(edge(one_last)):
            up[3 + i, mine, :] = v
    pl.when(me < n - 1)(ups[1].start)

    for x in range(rows):
        flat[pl.ds(x, count, stride=rows), :] = placed(got, x)
    tab[...] = flat[...].reshape(tab.shape)
    loads[2].wait()
    lax.fori_loop(0, me, lambda peer, _: greet(here, peer), None)
    fw_load.wait()

    def lower(values):
        return values - jnp.where(at_row == 0, 0.0, pltpu.roll(values, 1, 0))

    def upper(values):
        return jnp.where(at_row == last, 0.0, pltpu.roll(values, last, 0)) - values

    def pair(i, totals):
        perm, poro = totals
        both = pl.ds(pl.multiple_of(i * 2 * rows, 2 * rows), 2 * rows)
        stored = [fw[k, both, :].astype(jnp.float32) for k in range(6)]
        for k in range(6):
            wide[k, both, :] = stored[k]
        for half in range(2):
            e = i * 2 + half
            at = pl.ds(pl.multiple_of(e * rows, rows), rows)
            own = slice(half * rows, (half + 1) * rows)
            source = sid_ref[e]
            fields = [st[f, at, :] for f in range(8)]
            for t in range(2):
                forcing = [tab[(t * 2 + c) * sources + source] for c in range(2)]
                fields = velocity(fields, [lower(v) for v in edge(fields)], vel, lane, forcing)
                perm = perm + fields[QX] * stored[3 * t][own] + fields[QZ] * stored[3 * t + 1][own]
                fields = stress(fields, [upper(v) for v in front(fields)], coeffs, lane)
                poro = poro + fields[PR] * stored[3 * t + 2][own]
            for f in range(8):
                out_ref[f, at, :] = fields[f]
        return perm, poro

    perm, poro = lax.fori_loop(0, events // 2, pair, (zero, zero), unroll=12)

    pl.when(me > 0)(downs[2].start)
    has_low = jnp.where(me > 0, 1.0, 0.0)
    has_high = jnp.where(me < n - 1, 1.0, 0.0)

    def seen(b, k, x):
        return wide[k, pl.ds(b * 8 * rows + x, 8, stride=rows), :]

    def add(b, x, names, values):
        for f, v in zip(names, values):
            keep[slot_of[x] + f, own_block(b), :] = v

    pl.when(me > 0)(ups[0].wait_recv)
    pl.when(me < n - 1)(downs[0].wait_recv)
    for b in blocks:
        mine = own_block(b)
        one = velocity_share([low[i, mine, :] for i in range(3)], vel)
        perm = perm + one[QX] * seen(b, 0, 0) + one[QZ] * seen(b, 1, 0)
        met = plus([down[i, mine, :] for i in range(3)], front(one))
        rim = [v * has_low for v in beyond_share(met, coeffs)]
        two = one + stress_share(one, [-v for v in front(one)], coeffs, lane)
        poro = poro + two[PR] * seen(b, 2, 0)
        next_one = velocity_share(edge(two), vel)
        perm = perm + next_one[QX] * seen(b, 3, 1) + next_one[QZ] * seen(b, 4, 1)
        next_stress = stress_share(next_one, [-v for v in front(next_one)], coeffs, lane)
        poro = poro + next_stress[3] * seen(b, 5, 1)
        add(b, 1, range(8), next_one + next_stress)
        two = velocity(two, minus(edge(two), rim), vel, lane)
        add(b, 0, range(8), two)

        one = velocity_share([up[i, mine, :] for i in range(3)], vel)
        met = [(high[i, mine, :] + v) * has_high for i, v in enumerate(front(one))]
        own_stress = side_share(met, coeffs)
        poro = poro + own_stress[3] * seen(b, 2, last)
        two = one + stress_share(one, [-v for v in front(one)], coeffs, lane)
        full = plus([up[3 + i, mine, :] for i in range(3)], [own_stress[0], own_stress[2], own_stress[3]])
        two = velocity(two, minus(edge(two), full), vel, lane)
        beyond = [v * has_high for v in front(two)]
        own = velocity([zero] * 4 + own_stress, [own_stress[0], own_stress[2], own_stress[3]], vel, lane)
        perm = perm + own[QX] * seen(b, 3, last) + own[QZ] * seen(b, 4, last)
        prior = side_share(front(own), coeffs)
        own = stress(own, minus(beyond, front(own)), coeffs, lane)
        poro = poro + own[PR] * seen(b, 5, last) + prior[3] * seen(b, 5, last - 1)
        add(b, last, range(8), own)
        add(b, last - 1, range(XX, 8), prior)

    pl.when(me > 0)(ups[1].wait_recv)
    pl.when(me < n - 1)(downs[1].wait_recv)
    for b in blocks:
        mine = own_block(b)
        late = velocity_share([low[3 + i, mine, :] for i in range(3)], vel)
        two = [keep[slot_of[0] + f, mine, :] for f in range(8)]
        two = plus(two[:4], late) + two[4:]
        perm = perm + two[QX] * seen(b, 3, 0) + two[QZ] * seen(b, 4, 0)
        after = [keep[slot_of[1] + f, mine, :] for f in (VX, VZ, QX)]
        two = stress(two, minus(after, front(two)), coeffs, lane)
        poro = poro + two[PR] * seen(b, 5, 0)
        add(b, 0, range(8), two)
        poro = poro - high[3, mine, :] * seen(b, 5, last)

    totals = (perm, poro)
    sums[me] = jnp.concatenate([jnp.sum(total, axis=0, keepdims=True) for total in totals], axis=0)

    @pl.when(me < n - 1)
    def _():
        pl.semaphore_wait(here, n - 1 - me)

    def send(peer, _):
        @pl.when(peer != me)
        def _():
            pltpu.make_async_remote_copy(
                sums.at[me], sums.at[me], sum_send, sum_recv,
                device_id={"gx": peer}, device_id_type=pl.DeviceIdType.MESH,
            ).start()

    lax.fori_loop(0, n, send, None)
    pl.when(me < n - 1)(downs[2].wait_recv)
    for b in blocks:
        mine = own_block(b)
        beyond_x, beyond_z = high[4, mine, :], high[5, mine, :]
        beyond_flow = (high[3, mine, :] - coeffs[2] * beyond_x) / coeffs[3]
        late = side_share([beyond_x, beyond_z, beyond_flow], coeffs)[:3] + [-high[3, mine, :]]
        add(b, last, range(XX, 8), plus([keep[slot_of[last] + f, mine, :] for f in range(XX, 8)], late))
    for b in blocks:
        for x in (0, 1, last, last - 1):
            at = pl.ds(b * 8 * rows + x, 8, stride=rows)
            for f in range(XX if x == last - 1 else 0, 8):
                out_ref[f, at, :] = out_ref[f, at, :] + keep[slot_of[x] + f, b * 8 : (b + 1) * 8, :]
    pltpu.make_async_copy(sums.at[pl.ds(1, n - 1)], sums.at[pl.ds(0, n - 1)], sum_recv).wait()
    mine = jnp.sum(sums[...], axis=0)
    grad_ref[0:1, :] = vel[2] * vel[3] * mine[0:1] * scale
    grad_ref[1:2, :] = coeffs[3] * mine[1:2] * scale
    pltpu.make_async_copy(sums.at[pl.ds(1, n - 1)], sums.at[pl.ds(0, n - 1)], sum_send).wait()
    for copy in ups:
        pl.when(me < n - 1)(copy.wait_send)
    for copy in downs:
        pl.when(me > 0)(copy.wait_send)


def write(out_ref, grad_ref, out_hbm, grad_hbm, sems):
    fields = out_ref.shape[0]
    copies = [pltpu.make_async_copy(out_ref.at[f], out_hbm.at[f], sems.at[f]) for f in range(fields)]
    copies.append(pltpu.make_async_copy(grad_ref, grad_hbm, sems.at[fields]))
    for copy in copies:
        copy.start()
    for copy in copies:
        copy.wait()


def shards(adjoint_state, forward_fields, vel_coeffs, stress_coeffs, drm_cells, drm_force, source_id):
    fields, events, rows, depth = adjoint_state.shape
    cells = events * rows
    n = lax.axis_size("gx")
    scale = (events * rows * n) ** (-0.5)
    hbm, vmem = pl.BlockSpec(memory_space=pltpu.HBM), pl.BlockSpec(memory_space=pltpu.VMEM)
    f32 = jnp.float32
    dma = pltpu.SemaphoreType.DMA
    out, gradients = pl.pallas_call(
        functools.partial(kernel, n, scale),
        out_shape=[
            pltpu.VMEM((fields, cells, depth), f32),
            pltpu.VMEM((2, depth), f32),
        ],
        in_specs=[hbm] * 7,
        out_specs=[vmem, vmem],
        scratch_shapes=[
            pltpu.VMEM((fields, cells, depth), f32),
            pltpu.VMEM((6, cells, depth), jnp.bfloat16),
            pltpu.VMEM(vel_coeffs.shape, f32),
            pltpu.VMEM(stress_coeffs.shape, f32),
            pltpu.VMEM((1, drm_cells.shape[0]), jnp.int32),
            pltpu.VMEM(drm_force.shape, f32),
            pltpu.SMEM(source_id.shape, jnp.int32),
            pltpu.VMEM((4 * drm_force.shape[0] * rows, depth), f32),
            pltpu.VMEM((4 * drm_force.shape[0], rows, depth), f32),
            pltpu.VMEM((6, cells, depth), f32),
            pltpu.VMEM((32, events, depth), f32),
            pltpu.VMEM((6, events, depth), f32),
            pltpu.VMEM((6, events, depth), f32),
            pltpu.VMEM((6, events, depth), f32),
            pltpu.VMEM((6, events, depth), f32),
            pltpu.VMEM((n, 2, depth), f32),
            dma((3,)),
            dma,
            dma((5,)),
            dma((2, 2)),
            dma((2, 3)),
            dma,
            dma,
            pltpu.SemaphoreType.REGULAR,
        ],
        compiler_params=pltpu.CompilerParams(
            collective_id=0, has_side_effects=True
        ),
    )(
        adjoint_state.reshape(fields, cells, depth),
        forward_fields.reshape(6, cells, depth),
        vel_coeffs,
        stress_coeffs,
        drm_cells.reshape(1, -1),
        drm_force,
        source_id,
    )
    out, gradients = pl.pallas_call(
        write,
        out_shape=[jax.ShapeDtypeStruct(out.shape, f32), jax.ShapeDtypeStruct(gradients.shape, f32)],
        in_specs=[pl.BlockSpec(memory_space=pl.ANY)] * 2,
        out_specs=[hbm, hbm],
        scratch_shapes=[dma((fields + 1,))],
    )(pltpu.with_memory_space_constraint(out, pltpu.VMEM), pltpu.with_memory_space_constraint(gradients, pltpu.VMEM))
    return out.reshape(adjoint_state.shape), gradients


def solution(mesh):
    in_specs = (
        P(None, "groups", "gx", None),
        P(None, None, "groups", "gx", None),
        P("groups", None),
        P("groups", None),
        P("gx"),
        P("groups", None, None, "gx"),
        P("groups"),
    )
    out_specs = (P(None, "groups", "gx", None), P("groups", None))
    return jax.shard_map(shards, mesh=mesh, in_specs=in_specs, out_specs=out_specs, check_vma=False)
```

```python
import functools

import jax
import jax.numpy as jnp
from jax import lax
from jax.experimental import pallas as pl
from jax.experimental.pallas import tpu as pltpu
from jax.sharding import PartitionSpec as P

LAYER = 8
VX, VZ, QX, QZ, XX, ZZ, XZ, PR = range(8)


def coeff_rows(coeffs):
    return [coeffs[i : i + 1] for i in range(4)]


def depth_lower(values, lane):
    return values - jnp.where(lane == 0, 0.0, pltpu.roll(values, 1, 1))


def depth_upper(values, lane):
    last = values.shape[1] - 1
    return jnp.where(lane == last, 0.0, pltpu.roll(values, last, 1)) - values


def velocity(fields, sides, vel, lane, forcing=None):
    vel_x, vel_z, flow_x, flow_z, _, stress_zz, stress_xz, pressure = fields
    solid, couple, fluid, drag = vel
    force_x = sides[0] + depth_lower(stress_xz, lane)
    force_z = sides[1] + depth_lower(stress_zz, lane)
    push_x = sides[2] + drag * flow_x
    push_z = depth_lower(pressure, lane) + drag * flow_z
    new_x = vel_x + solid * force_x + couple * push_x
    new_z = vel_z + solid * force_z + couple * push_z
    if forcing is not None:
        new_x = new_x + forcing[0]
        new_z = new_z + forcing[1]
    flow_x = flow_x - couple * force_x - fluid * push_x
    flow_z = flow_z - couple * force_z - fluid * push_z
    return [new_x, new_z, flow_x, flow_z, *fields[4:]]


def stress(fields, sides, coeffs, lane):
    vel_x, vel_z, flow_x, flow_z, xx, zz, xz, pressure = fields
    lame, shear, couple, fluid = coeffs
    strain_z = depth_upper(vel_z, lane)
    dilation = sides[0] + strain_z
    inflow = sides[2] + depth_upper(flow_z, lane)
    shared = lame * dilation - couple * inflow
    twice = 2.0 * shear
    xx = xx + shared + twice * sides[0]
    zz = zz + shared + twice * strain_z
    xz = xz + shear * (depth_upper(vel_x, lane) + sides[1])
    pressure = pressure - couple * dilation - fluid * inflow
    return [vel_x, vel_z, flow_x, flow_z, xx, zz, xz, pressure]


def side_share(row, coeffs):
    lame, shear, couple, fluid = coeffs
    zz = lame * row[0] - couple * row[2]
    pressure = -couple * row[0] - fluid * row[2]
    return [zz + 2.0 * shear * row[0], zz, shear * row[1], pressure]


def beyond_share(row, coeffs):
    xx, _, xz, pressure = side_share(row, coeffs)
    return [xx, xz, pressure]


def velocity_share(row, vel):
    solid, couple, fluid, _ = vel
    xx, xz, pressure = row
    return [-(solid * xx + couple * pressure), -solid * xz, couple * xx + fluid * pressure, couple * xz]


def stress_share(moved, sides, coeffs, lane):
    vel_x, vel_z, flow_x, flow_z = moved
    lame, shear, couple, fluid = coeffs
    strain_z = depth_upper(vel_z, lane)
    dilation = sides[0] + strain_z
    inflow = sides[2] + depth_upper(flow_z, lane)
    shared = lame * dilation - couple * inflow
    twice = 2.0 * shear
    return [
        shared + twice * sides[0],
        shared + twice * strain_z,
        shear * (depth_upper(vel_x, lane) + sides[1]),
        -couple * dilation - fluid * inflow,
    ]


def edge(fields):
    return [fields[XX], fields[XZ], fields[PR]]


def front(fields):
    return [fields[VX], fields[VZ], fields[QX]]


def minus(first, second):
    return [a - b for a, b in zip(first, second)]


def plus(first, second):
    return [a + b for a, b in zip(first, second)]


def kernel(
    n, scale, st_hbm, fw_hbm, vc_hbm, sc_hbm, cell_hbm, df_hbm, sid_hbm, out_ref, grad_ref,
    st, fw, vc_ref, sc_ref, cell_ref, df_ref, sid_ref, flat, tab, wide, keep, up, down, low, high, sums,
    st_sem, fw_sem, small_sem, up_sem, down_sem, sum_send, sum_recv, here,
):
    _, cells, depth = st.shape
    events = up.shape[1]
    rows = cells // events
    sources = df_ref.shape[0]
    me = lax.axis_index("gx")
    barrier = pltpu.get_barrier_semaphore()

    def greet(semaphore, peer):
        pl.semaphore_signal(semaphore, inc=1, device_id={"gx": peer}, device_id_type=pl.DeviceIdType.MESH)

    @pl.when(me > 0)
    def _():
        greet(barrier, me - 1)

    @pl.when(me < n - 1)
    def _():
        greet(barrier, me + 1)

    smalls = [
        pltpu.make_async_copy(src, dst, small_sem.at[i])
        for i, (src, dst) in enumerate(
            [(df_hbm, df_ref), (cell_hbm, cell_ref), (sid_hbm, sid_ref), (vc_hbm, vc_ref), (sc_hbm, sc_ref)]
        )
    ]
    for small in smalls:
        small.start()
    last = rows - 1
    from_hbm, to_vmem = st_hbm.reshape(8, events, rows, depth), st.reshape(8, events, rows, depth)
    loads = [
        pltpu.make_async_copy(from_hbm.at[:, :, at], to_vmem.at[:, :, at], st_sem.at[i])
        for i, at in enumerate([pl.ds(0, 2), pl.ds(last - 1, 2), pl.ds(2, rows - 4)])
    ]
    loads[0].start()
    loads[1].start()
    fw_load = pltpu.make_async_copy(fw_hbm, fw, fw_sem)
    lax.fori_loop(me + 2, n, lambda peer, _: greet(barrier, peer), None)

    @pl.when(me == 0)
    def _():
        low[...] = jnp.zeros(low.shape, jnp.float32)

    @pl.when(me == n - 1)
    def _():
        high[...] = jnp.zeros(high.shape, jnp.float32)

    for small in smalls:
        small.wait()
    vel = coeff_rows(vc_ref[...])
    coeffs = coeff_rows(sc_ref[...])

    def three(values):
        first = values.astype(jnp.bfloat16)
        rest = values - first.astype(jnp.float32)
        second = rest.astype(jnp.bfloat16)
        return [first, second, (rest - second.astype(jnp.float32)).astype(jnp.bfloat16)]

    force = jnp.concatenate([df_ref[:, t, c, :] for t in range(2) for c in range(2)], axis=0)
    count = force.shape[0]
    place = cell_ref[...] - me * (rows * depth)
    column = lax.broadcasted_iota(jnp.int32, (depth, place.shape[1]), 0)
    spot = (column // LAYER) * depth + (depth - LAYER) + lax.rem(column, LAYER)
    hot = jnp.where(spot == place, 1.0, 0.0).astype(jnp.bfloat16)
    got = lax.dot_general(
        jnp.concatenate(three(force), axis=0), hot, (((1,), (1,)), ((), ())), preferred_element_type=jnp.float32
    )
    got = got[:count] + got[count : 2 * count] + got[2 * count :]

    def placed(values, x):
        at = lax.broadcasted_iota(jnp.int32, values.shape, 1)
        return jnp.where(at < depth - LAYER, 0.0, pltpu.roll(values, depth - LAYER - x * LAYER, 1))

    row_id = lax.broadcasted_iota(jnp.int32, (8, sources), 0)
    source_at = lax.broadcasted_iota(jnp.int32, (8, sources), 1)
    blocks = []
    for b in range(events // 8):
        wanted = jnp.full((8, sources), sid_ref[b * 8], jnp.int32)
        for r in range(1, 8):
            wanted = jnp.where(row_id == r, sid_ref[b * 8 + r], wanted)
        blocks.append(jnp.where(wanted == source_at, 1.0, 0.0))
    picked = jnp.concatenate(blocks, axis=0).astype(jnp.bfloat16)
    picked = jnp.concatenate([picked] * 3, axis=1)

    def event_forcing(t):
        return [
            jnp.dot(
                picked, jnp.concatenate(three(got[(t * 2 + c) * sources : (t * 2 + c + 1) * sources]), axis=0),
                preferred_element_type=jnp.float32,
            )
            for c in range(2)
        ]

    slot_of = {0: 0, 1: 8, last: 16, last - 1: 24}
    now, later = event_forcing(0), event_forcing(1)
    force_0, force_1, force_last = [[placed(v, x) for v in now] for x in (0, 1, last)]
    later_0 = [placed(v, 0) for v in later]

    lane = lax.broadcasted_iota(jnp.int32, (8, depth), 1)
    at_row = lax.broadcasted_iota(jnp.int32, (rows, depth), 0)
    zero = jnp.zeros((8, depth), jnp.float32)
    blocks = range(events // 8)

    ups, downs = [], []
    for c in range(2):
        half = pl.ds(3 * c, 3)
        ups.append(
            pltpu.make_async_remote_copy(
                up.at[half], low.at[half], up_sem.at[0, c], up_sem.at[1, c],
                device_id={"gx": jnp.minimum(me + 1, n - 1)}, device_id_type=pl.DeviceIdType.MESH,
            )
        )
    for c, part in enumerate([pl.ds(0, 3), pl.ds(3, 1), pl.ds(4, 2)]):
        downs.append(
            pltpu.make_async_remote_copy(
                down.at[part], high.at[part], down_sem.at[0, c], down_sem.at[1, c],
                device_id={"gx": jnp.maximum(me - 1, 0)}, device_id_type=pl.DeviceIdType.MESH,
            )
        )

    def own_block(b):
        return slice(b * 8, (b + 1) * 8)

    def row(b, x, names=range(8)):
        return [st[f, pl.ds(b * 8 * rows + x, 8, stride=rows), :] for f in names]

    loads[0].wait()
    loads[2].start()
    fw_load.start()
    firsts = []
    for b in blocks:
        row_0 = row(b, 0)
        one_0 = velocity(row_0, edge(row_0), vel, lane, [v[own_block(b)] for v in force_0])
        for i, v in enumerate(front(one_0)):
            down[i, own_block(b), :] = v
        firsts.append(one_0)
    pl.semaphore_wait(barrier, me + jnp.where(me < n - 1, 1, 0))
    pl.when(me > 0)(downs[0].start)
    loads[1].wait()
    for b in blocks:
        for i, v in enumerate(row(b, last, (XX, XZ, PR))):
            up[i, own_block(b), :] = v
    pl.when(me < n - 1)(ups[0].start)
    for b in blocks:
        mine = own_block(b)
        row_0, row_1, one_0 = row(b, 0, (XX, XZ, PR)), row(b, 1), firsts[b]
        one_1 = velocity(row_1, minus(edge(row_1), row_0), vel, lane, [v[mine] for v in force_1])
        two_0 = stress(one_0, minus(front(one_1), front(one_0)), coeffs, lane)
        two_0 = velocity(two_0, edge(two_0), vel, lane, [v[mine] for v in later_0])
        down[3, mine, :] = coeffs[2] * two_0[VX] + coeffs[3] * two_0[QX]
        down[4, mine, :] = two_0[VX]
        down[5, mine, :] = two_0[VZ]
    pl.when(me > 0)(downs[1].start)
    for b in blocks:
        mine = own_block(b)
        row_last = row(b, last)
        sides = minus(edge(row_last), row(b, last - 1, (XX, XZ, PR)))
        one_last = velocity(row_last, sides, vel, lane, [v[mine] for v in force_last])
        one_last = stress(one_last, [-v for v in front(one_last)], coeffs, lane)
        for i, v in enumerate(edge(one_last)):
            up[3 + i, mine, :] = v
    pl.when(me < n - 1)(ups[1].start)

    for x in range(rows):
        flat[pl.ds(x, count, stride=rows), :] = placed(got, x)
    tab[...] = flat[...].reshape(tab.shape)
    loads[2].wait()
    lax.fori_loop(0, me, lambda peer, _: greet(here, peer), None)
    fw_load.wait()

    def lower(values):
        return values - jnp.where(at_row == 0, 0.0, pltpu.roll(values, 1, 0))

    def upper(values):
        return jnp.where(at_row == last, 0.0, pltpu.roll(values, last, 0)) - values

    def pair(i, totals):
        perm, poro = totals
        both = pl.ds(pl.multiple_of(i * 2 * rows, 2 * rows), 2 * rows)
        stored = [fw[k, both, :].astype(jnp.float32) for k in range(6)]
        for k in range(6):
            wide[k, both, :] = stored[k]
        for half in range(2):
            e = i * 2 + half
            at = pl.ds(pl.multiple_of(e * rows, rows), rows)
            own = slice(half * rows, (half + 1) * rows)
            source = sid_ref[e]
            fields = [st[f, at, :] for f in range(8)]
            for t in range(2):
                forcing = [tab[(t * 2 + c) * sources + source] for c in range(2)]
                fields = velocity(fields, [lower(v) for v in edge(fields)], vel, lane, forcing)
                perm = perm + fields[QX] * stored[3 * t][own] + fields[QZ] * stored[3 * t + 1][own]
                fields = stress(fields, [upper(v) for v in front(fields)], coeffs, lane)
                poro = poro + fields[PR] * stored[3 * t + 2][own]
            for f in range(8):
                out_ref[f, at, :] = fields[f]
        return perm, poro

    perm, poro = lax.fori_loop(0, events // 2, pair, (zero, zero), unroll=12)

    pl.when(me > 0)(downs[2].start)
    has_low = jnp.where(me > 0, 1.0, 0.0)
    has_high = jnp.where(me < n - 1, 1.0, 0.0)

    def seen(b, k, x):
        return wide[k, pl.ds(b * 8 * rows + x, 8, stride=rows), :]

    def add(b, x, names, values):
        for f, v in zip(names, values):
            keep[slot_of[x] + f, own_block(b), :] = v

    pl.when(me > 0)(ups[0].wait_recv)
    pl.when(me < n - 1)(downs[0].wait_recv)
    for b in blocks:
        mine = own_block(b)
        one = velocity_share([low[i, mine, :] for i in range(3)], vel)
        perm = perm + one[QX] * seen(b, 0, 0) + one[QZ] * seen(b, 1, 0)
        met = plus([down[i, mine, :] for i in range(3)], front(one))
        rim = [v * has_low for v in beyond_share(met, coeffs)]
        two = one + stress_share(one, [-v for v in front(one)], coeffs, lane)
        poro = poro + two[PR] * seen(b, 2, 0)
        next_one = velocity_share(edge(two), vel)
        perm = perm + next_one[QX] * seen(b, 3, 1) + next_one[QZ] * seen(b, 4, 1)
        next_stress = stress_share(next_one, [-v for v in front(next_one)], coeffs, lane)
        poro = poro + next_stress[3] * seen(b, 5, 1)
        add(b, 1, range(8), next_one + next_stress)
        two = velocity(two, minus(edge(two), rim), vel, lane)
        add(b, 0, range(8), two)

        one = velocity_share([up[i, mine, :] for i in range(3)], vel)
        met = [(high[i, mine, :] + v) * has_high for i, v in enumerate(front(one))]
        own_stress = side_share(met, coeffs)
        poro = poro + own_stress[3] * seen(b, 2, last)
        two = one + stress_share(one, [-v for v in front(one)], coeffs, lane)
        full = plus([up[3 + i, mine, :] for i in range(3)], [own_stress[0], own_stress[2], own_stress[3]])
        two = velocity(two, minus(edge(two), full), vel, lane)
        beyond = [v * has_high for v in front(two)]
        own = velocity([zero] * 4 + own_stress, [own_stress[0], own_stress[2], own_stress[3]], vel, lane)
        perm = perm + own[QX] * seen(b, 3, last) + own[QZ] * seen(b, 4, last)
        prior = side_share(front(own), coeffs)
        own = stress(own, minus(beyond, front(own)), coeffs, lane)
        poro = poro + own[PR] * seen(b, 5, last) + prior[3] * seen(b, 5, last - 1)
        add(b, last, range(8), own)
        add(b, last - 1, range(XX, 8), prior)

    pl.when(me > 0)(ups[1].wait_recv)
    pl.when(me < n - 1)(downs[1].wait_recv)
    for b in blocks:
        mine = own_block(b)
        late = velocity_share([low[3 + i, mine, :] for i in range(3)], vel)
        two = [keep[slot_of[0] + f, mine, :] for f in range(8)]
        two = plus(two[:4], late) + two[4:]
        perm = perm + two[QX] * seen(b, 3, 0) + two[QZ] * seen(b, 4, 0)
        after = [keep[slot_of[1] + f, mine, :] for f in (VX, VZ, QX)]
        two = stress(two, minus(after, front(two)), coeffs, lane)
        poro = poro + two[PR] * seen(b, 5, 0)
        add(b, 0, range(8), two)
        poro = poro - high[3, mine, :] * seen(b, 5, last)

    totals = (perm, poro)
    sums[me] = jnp.concatenate([jnp.sum(total, axis=0, keepdims=True) for total in totals], axis=0)

    @pl.when(me < n - 1)
    def _():
        pl.semaphore_wait(here, n - 1 - me)

    def send(peer, _):
        @pl.when(peer != me)
        def _():
            pltpu.make_async_remote_copy(
                sums.at[me], sums.at[me], sum_send, sum_recv,
                device_id={"gx": peer}, device_id_type=pl.DeviceIdType.MESH,
            ).start()

    lax.fori_loop(0, n, send, None)
    pl.when(me < n - 1)(downs[2].wait_recv)
    for b in blocks:
        mine = own_block(b)
        beyond_x, beyond_z = high[4, mine, :], high[5, mine, :]
        beyond_flow = (high[3, mine, :] - coeffs[2] * beyond_x) / coeffs[3]
        late = side_share([beyond_x, beyond_z, beyond_flow], coeffs)[:3] + [-high[3, mine, :]]
        add(b, last, range(XX, 8), plus([keep[slot_of[last] + f, mine, :] for f in range(XX, 8)], late))
    for b in blocks:
        for x in (0, 1, last, last - 1):
            at = pl.ds(b * 8 * rows + x, 8, stride=rows)
            for f in range(XX if x == last - 1 else 0, 8):
                out_ref[f, at, :] = out_ref[f, at, :] + keep[slot_of[x] + f, b * 8 : (b + 1) * 8, :]
    pltpu.make_async_copy(sums.at[pl.ds(1, n - 1)], sums.at[pl.ds(0, n - 1)], sum_recv).wait()
    mine = jnp.sum(sums[...], axis=0)
    grad_ref[0:1, :] = vel[2] * vel[3] * mine[0:1] * scale
    grad_ref[1:2, :] = coeffs[3] * mine[1:2] * scale
    pltpu.make_async_copy(sums.at[pl.ds(1, n - 1)], sums.at[pl.ds(0, n - 1)], sum_send).wait()
    for copy in ups:
        pl.when(me < n - 1)(copy.wait_send)
    for copy in downs:
        pl.when(me > 0)(copy.wait_send)


def write(out_ref, grad_ref, out_hbm, grad_hbm, sems):
    fields = out_ref.shape[0]
    copies = [pltpu.make_async_copy(out_ref.at[f], out_hbm.at[f], sems.at[f]) for f in range(fields)]
    copies.append(pltpu.make_async_copy(grad_ref, grad_hbm, sems.at[fields]))
    for copy in copies:
        copy.start()
    for copy in copies:
        copy.wait()


def shards(adjoint_state, forward_fields, vel_coeffs, stress_coeffs, drm_cells, drm_force, source_id):
    fields, events, rows, depth = adjoint_state.shape
    cells = events * rows
    n = lax.axis_size("gx")
    scale = (events * rows * n) ** (-0.5)
    hbm, vmem = pl.BlockSpec(memory_space=pltpu.HBM), pl.BlockSpec(memory_space=pltpu.VMEM)
    f32 = jnp.float32
    dma = pltpu.SemaphoreType.DMA
    out, gradients = pl.pallas_call(
        functools.partial(kernel, n, scale),
        out_shape=[
            pltpu.VMEM((fields, cells, depth), f32),
            pltpu.VMEM((2, depth), f32),
        ],
        in_specs=[hbm] * 7,
        out_specs=[vmem, vmem],
        scratch_shapes=[
            pltpu.VMEM((fields, cells, depth), f32),
            pltpu.VMEM((6, cells, depth), jnp.bfloat16),
            pltpu.VMEM(vel_coeffs.shape, f32),
            pltpu.VMEM(stress_coeffs.shape, f32),
            pltpu.VMEM((1, drm_cells.shape[0]), jnp.int32),
            pltpu.VMEM(drm_force.shape, f32),
            pltpu.SMEM(source_id.shape, jnp.int32),
            pltpu.VMEM((4 * drm_force.shape[0] * rows, depth), f32),
            pltpu.VMEM((4 * drm_force.shape[0], rows, depth), f32),
            pltpu.VMEM((6, cells, depth), f32),
            pltpu.VMEM((32, events, depth), f32),
            pltpu.VMEM((6, events, depth), f32),
            pltpu.VMEM((6, events, depth), f32),
            pltpu.VMEM((6, events, depth), f32),
            pltpu.VMEM((6, events, depth), f32),
            pltpu.VMEM((n, 2, depth), f32),
            dma((3,)),
            dma,
            dma((5,)),
            dma((2, 2)),
            dma((2, 3)),
            dma,
            dma,
            pltpu.SemaphoreType.REGULAR,
        ],
        compiler_params=pltpu.CompilerParams(
            collective_id=0, has_side_effects=True
        ),
    )(
        adjoint_state.reshape(fields, cells, depth),
        forward_fields.reshape(6, cells, depth),
        vel_coeffs,
        stress_coeffs,
        drm_cells.reshape(1, -1),
        drm_force,
        source_id,
    )
    out, gradients = pl.pallas_call(
        write,
        out_shape=[jax.ShapeDtypeStruct(out.shape, f32), jax.ShapeDtypeStruct(gradients.shape, f32)],
        in_specs=[pl.BlockSpec(memory_space=pl.ANY)] * 2,
        out_specs=[hbm, hbm],
        scratch_shapes=[dma((fields + 1,))],
    )(pltpu.with_memory_space_constraint(out, pltpu.VMEM), pltpu.with_memory_space_constraint(gradients, pltpu.VMEM))
    return out.reshape(adjoint_state.shape), gradients


def solution(mesh):
    in_specs = (
        P(None, "groups", "gx", None),
        P(None, None, "groups", "gx", None),
        P("groups", None),
        P("groups", None),
        P("gx"),
        P("groups", None, None, "gx"),
        P("groups"),
    )
    out_specs = (P(None, "groups", "gx", None), P("groups", None))
    return jax.shard_map(shards, mesh=mesh, in_specs=in_specs, out_specs=out_specs, check_vma=False)
```

```python
import functools

import jax
import jax.numpy as jnp
from jax import lax
from jax.experimental import pallas as pl
from jax.experimental.pallas import tpu as pltpu
from jax.sharding import PartitionSpec as P

LAYER = 8
VX, VZ, QX, QZ, XX, ZZ, XZ, PR = range(8)


def coeff_rows(coeffs):
    return [coeffs[i : i + 1] for i in range(4)]


def depth_lower(values, lane):
    return values - jnp.where(lane == 0, 0.0, pltpu.roll(values, 1, 1))


def depth_upper(values, lane):
    last = values.shape[1] - 1
    return jnp.where(lane == last, 0.0, pltpu.roll(values, last, 1)) - values


def velocity(fields, sides, vel, lane, forcing=None):
    vel_x, vel_z, flow_x, flow_z, _, stress_zz, stress_xz, pressure = fields
    solid, couple, fluid, drag = vel
    force_x = sides[0] + depth_lower(stress_xz, lane)
    force_z = sides[1] + depth_lower(stress_zz, lane)
    push_x = sides[2] + drag * flow_x
    push_z = depth_lower(pressure, lane) + drag * flow_z
    new_x = vel_x + solid * force_x + couple * push_x
    new_z = vel_z + solid * force_z + couple * push_z
    if forcing is not None:
        new_x = new_x + forcing[0]
        new_z = new_z + forcing[1]
    flow_x = flow_x - couple * force_x - fluid * push_x
    flow_z = flow_z - couple * force_z - fluid * push_z
    return [new_x, new_z, flow_x, flow_z, *fields[4:]]


def stress(fields, sides, coeffs, lane):
    vel_x, vel_z, flow_x, flow_z, xx, zz, xz, pressure = fields
    lame, shear, couple, fluid = coeffs
    strain_z = depth_upper(vel_z, lane)
    dilation = sides[0] + strain_z
    inflow = sides[2] + depth_upper(flow_z, lane)
    shared = lame * dilation - couple * inflow
    twice = 2.0 * shear
    xx = xx + shared + twice * sides[0]
    zz = zz + shared + twice * strain_z
    xz = xz + shear * (depth_upper(vel_x, lane) + sides[1])
    pressure = pressure - couple * dilation - fluid * inflow
    return [vel_x, vel_z, flow_x, flow_z, xx, zz, xz, pressure]


def side_share(row, coeffs):
    lame, shear, couple, fluid = coeffs
    zz = lame * row[0] - couple * row[2]
    pressure = -couple * row[0] - fluid * row[2]
    return [zz + 2.0 * shear * row[0], zz, shear * row[1], pressure]


def beyond_share(row, coeffs):
    xx, _, xz, pressure = side_share(row, coeffs)
    return [xx, xz, pressure]


def velocity_share(row, vel):
    solid, couple, fluid, _ = vel
    xx, xz, pressure = row
    return [-(solid * xx + couple * pressure), -solid * xz, couple * xx + fluid * pressure, couple * xz]


def stress_share(moved, sides, coeffs, lane):
    vel_x, vel_z, flow_x, flow_z = moved
    lame, shear, couple, fluid = coeffs
    strain_z = depth_upper(vel_z, lane)
    dilation = sides[0] + strain_z
    inflow = sides[2] + depth_upper(flow_z, lane)
    shared = lame * dilation - couple * inflow
    twice = 2.0 * shear
    return [
        shared + twice * sides[0],
        shared + twice * strain_z,
        shear * (depth_upper(vel_x, lane) + sides[1]),
        -couple * dilation - fluid * inflow,
    ]


def edge(fields):
    return [fields[XX], fields[XZ], fields[PR]]


def front(fields):
    return [fields[VX], fields[VZ], fields[QX]]


def minus(first, second):
    return [a - b for a, b in zip(first, second)]


def plus(first, second):
    return [a + b for a, b in zip(first, second)]


def kernel(
    n, scale, st_hbm, fw_hbm, vc_hbm, sc_hbm, cell_hbm, df_hbm, sid_hbm, out_ref, sums_ref, factor_ref,
    st, fw, vc_ref, sc_ref, cell_ref, df_ref, sid_ref, flat, tab, wide, keep, up, down, low, high, sums,
    st_sem, fw_sem, small_sem, up_sem, down_sem, sum_send, sum_recv, here,
):
    _, cells, depth = st.shape
    events = up.shape[1]
    rows = cells // events
    sources = df_ref.shape[0]
    me = lax.axis_index("gx")
    barrier = pltpu.get_barrier_semaphore()

    def greet(semaphore, peer):
        pl.semaphore_signal(semaphore, inc=1, device_id={"gx": peer}, device_id_type=pl.DeviceIdType.MESH)

    @pl.when(me > 0)
    def _():
        greet(barrier, me - 1)

    @pl.when(me < n - 1)
    def _():
        greet(barrier, me + 1)

    smalls = [
        pltpu.make_async_copy(src, dst, small_sem.at[i])
        for i, (src, dst) in enumerate(
            [(df_hbm, df_ref), (cell_hbm, cell_ref), (sid_hbm, sid_ref), (vc_hbm, vc_ref), (sc_hbm, sc_ref)]
        )
    ]
    for small in smalls:
        small.start()
    last = rows - 1
    from_hbm, to_vmem = st_hbm.reshape(8, events, rows, depth), st.reshape(8, events, rows, depth)
    loads = [
        pltpu.make_async_copy(from_hbm.at[:, :, at], to_vmem.at[:, :, at], st_sem.at[i])
        for i, at in enumerate([pl.ds(0, 2), pl.ds(last - 1, 2), pl.ds(2, rows - 4)])
    ]
    loads[0].start()
    loads[1].start()
    fw_load = pltpu.make_async_copy(fw_hbm, fw, fw_sem)
    lax.fori_loop(me + 2, n, lambda peer, _: greet(barrier, peer), None)

    @pl.when(me == 0)
    def _():
        low[...] = jnp.zeros(low.shape, jnp.float32)

    @pl.when(me == n - 1)
    def _():
        high[...] = jnp.zeros(high.shape, jnp.float32)

    for small in smalls:
        small.wait()
    vel = coeff_rows(vc_ref[...])
    coeffs = coeff_rows(sc_ref[...])

    def three(values):
        first = values.astype(jnp.bfloat16)
        rest = values - first.astype(jnp.float32)
        second = rest.astype(jnp.bfloat16)
        return [first, second, (rest - second.astype(jnp.float32)).astype(jnp.bfloat16)]

    force = jnp.concatenate([df_ref[:, t, c, :] for t in range(2) for c in range(2)], axis=0)
    count = force.shape[0]
    place = cell_ref[...] - me * (rows * depth)
    column = lax.broadcasted_iota(jnp.int32, (depth, place.shape[1]), 0)
    spot = (column // LAYER) * depth + (depth - LAYER) + lax.rem(column, LAYER)
    hot = jnp.where(spot == place, 1.0, 0.0).astype(jnp.bfloat16)
    got = lax.dot_general(
        jnp.concatenate(three(force), axis=0), hot, (((1,), (1,)), ((), ())), preferred_element_type=jnp.float32
    )
    got = got[:count] + got[count : 2 * count] + got[2 * count :]

    def placed(values, x):
        at = lax.broadcasted_iota(jnp.int32, values.shape, 1)
        return jnp.where(at < depth - LAYER, 0.0, pltpu.roll(values, depth - LAYER - x * LAYER, 1))

    row_id = lax.broadcasted_iota(jnp.int32, (8, sources), 0)
    source_at = lax.broadcasted_iota(jnp.int32, (8, sources), 1)
    blocks = []
    for b in range(events // 8):
        wanted = jnp.full((8, sources), sid_ref[b * 8], jnp.int32)
        for r in range(1, 8):
            wanted = jnp.where(row_id == r, sid_ref[b * 8 + r], wanted)
        blocks.append(jnp.where(wanted == source_at, 1.0, 0.0))
    picked = jnp.concatenate(blocks, axis=0).astype(jnp.bfloat16)
    picked = jnp.concatenate([picked] * 3, axis=1)

    def event_forcing(t):
        return [
            jnp.dot(
                picked, jnp.concatenate(three(got[(t * 2 + c) * sources : (t * 2 + c + 1) * sources]), axis=0),
                preferred_element_type=jnp.float32,
            )
            for c in range(2)
        ]

    slot_of = {0: 0, 1: 8, last: 16, last - 1: 24}
    now, later = event_forcing(0), event_forcing(1)
    force_0, force_1, force_last = [[placed(v, x) for v in now] for x in (0, 1, last)]
    later_0 = [placed(v, 0) for v in later]

    lane = lax.broadcasted_iota(jnp.int32, (8, depth), 1)
    at_row = lax.broadcasted_iota(jnp.int32, (rows, depth), 0)
    zero = jnp.zeros((8, depth), jnp.float32)
    blocks = range(events // 8)

    ups, downs = [], []
    for c in range(2):
        half = pl.ds(3 * c, 3)
        ups.append(
            pltpu.make_async_remote_copy(
                up.at[half], low.at[half], up_sem.at[0, c], up_sem.at[1, c],
                device_id={"gx": jnp.minimum(me + 1, n - 1)}, device_id_type=pl.DeviceIdType.MESH,
            )
        )
    for c, part in enumerate([pl.ds(0, 3), pl.ds(3, 1), pl.ds(4, 2)]):
        downs.append(
            pltpu.make_async_remote_copy(
                down.at[part], high.at[part], down_sem.at[0, c], down_sem.at[1, c],
                device_id={"gx": jnp.maximum(me - 1, 0)}, device_id_type=pl.DeviceIdType.MESH,
            )
        )

    def own_block(b):
        return slice(b * 8, (b + 1) * 8)

    def row(b, x, names=range(8)):
        return [st[f, pl.ds(b * 8 * rows + x, 8, stride=rows), :] for f in names]

    loads[0].wait()
    loads[2].start()
    fw_load.start()
    firsts = []
    for b in blocks:
        row_0 = row(b, 0)
        one_0 = velocity(row_0, edge(row_0), vel, lane, [v[own_block(b)] for v in force_0])
        for i, v in enumerate(front(one_0)):
            down[i, own_block(b), :] = v
        firsts.append(one_0)
    pl.semaphore_wait(barrier, me + jnp.where(me < n - 1, 1, 0))
    pl.when(me > 0)(downs[0].start)
    loads[1].wait()
    for b in blocks:
        for i, v in enumerate(row(b, last, (XX, XZ, PR))):
            up[i, own_block(b), :] = v
    pl.when(me < n - 1)(ups[0].start)
    for b in blocks:
        mine = own_block(b)
        row_0, row_1, one_0 = row(b, 0, (XX, XZ, PR)), row(b, 1), firsts[b]
        one_1 = velocity(row_1, minus(edge(row_1), row_0), vel, lane, [v[mine] for v in force_1])
        two_0 = stress(one_0, minus(front(one_1), front(one_0)), coeffs, lane)
        two_0 = velocity(two_0, edge(two_0), vel, lane, [v[mine] for v in later_0])
        down[3, mine, :] = coeffs[2] * two_0[VX] + coeffs[3] * two_0[QX]
        down[4, mine, :] = two_0[VX]
        down[5, mine, :] = two_0[VZ]
    pl.when(me > 0)(downs[1].start)
    for b in blocks:
        mine = own_block(b)
        row_last = row(b, last)
        sides = minus(edge(row_last), row(b, last - 1, (XX, XZ, PR)))
        one_last = velocity(row_last, sides, vel, lane, [v[mine] for v in force_last])
        one_last = stress(one_last, [-v for v in front(one_last)], coeffs, lane)
        for i, v in enumerate(edge(one_last)):
            up[3 + i, mine, :] = v
    pl.when(me < n - 1)(ups[1].start)

    for x in range(rows):
        flat[pl.ds(x, count, stride=rows), :] = placed(got, x)
    tab[...] = flat[...].reshape(tab.shape)
    loads[2].wait()
    lax.fori_loop(0, me, lambda peer, _: greet(here, peer), None)
    fw_load.wait()
    factor_ref[0:1, :] = vel[2] * vel[3] * scale
    factor_ref[1:2, :] = coeffs[3] * scale

    def lower(values):
        return values - jnp.where(at_row == 0, 0.0, pltpu.roll(values, 1, 0))

    def upper(values):
        return jnp.where(at_row == last, 0.0, pltpu.roll(values, last, 0)) - values

    def pair(i, totals):
        perm, poro = totals
        both = pl.ds(pl.multiple_of(i * 2 * rows, 2 * rows), 2 * rows)
        stored = [fw[k, both, :].astype(jnp.float32) for k in range(6)]
        for k in range(6):
            wide[k, both, :] = stored[k]
        for half in range(2):
            e = i * 2 + half
            at = pl.ds(pl.multiple_of(e * rows, rows), rows)
            own = slice(half * rows, (half + 1) * rows)
            source = sid_ref[e]
            fields = [st[f, at, :] for f in range(8)]
            for t in range(2):
                forcing = [tab[(t * 2 + c) * sources + source] for c in range(2)]
                fields = velocity(fields, [lower(v) for v in edge(fields)], vel, lane, forcing)
                perm = perm + fields[QX] * stored[3 * t][own] + fields[QZ] * stored[3 * t + 1][own]
                fields = stress(fields, [upper(v) for v in front(fields)], coeffs, lane)
                poro = poro + fields[PR] * stored[3 * t + 2][own]
            for f in range(8):
                out_ref[f, at, :] = fields[f]
        return perm, poro

    perm, poro = lax.fori_loop(0, events // 2, pair, (zero, zero), unroll=12)

    pl.when(me > 0)(downs[2].start)
    has_low = jnp.where(me > 0, 1.0, 0.0)
    has_high = jnp.where(me < n - 1, 1.0, 0.0)

    def seen(b, k, x):
        return wide[k, pl.ds(b * 8 * rows + x, 8, stride=rows), :]

    def add(b, x, names, values):
        for f, v in zip(names, values):
            keep[slot_of[x] + f, own_block(b), :] = v

    pl.when(me > 0)(ups[0].wait_recv)
    pl.when(me < n - 1)(downs[0].wait_recv)
    for b in blocks:
        mine = own_block(b)
        one = velocity_share([low[i, mine, :] for i in range(3)], vel)
        perm = perm + one[QX] * seen(b, 0, 0) + one[QZ] * seen(b, 1, 0)
        met = plus([down[i, mine, :] for i in range(3)], front(one))
        rim = [v * has_low for v in beyond_share(met, coeffs)]
        two = one + stress_share(one, [-v for v in front(one)], coeffs, lane)
        poro = poro + two[PR] * seen(b, 2, 0)
        next_one = velocity_share(edge(two), vel)
        perm = perm + next_one[QX] * seen(b, 3, 1) + next_one[QZ] * seen(b, 4, 1)
        next_stress = stress_share(next_one, [-v for v in front(next_one)], coeffs, lane)
        poro = poro + next_stress[3] * seen(b, 5, 1)
        add(b, 1, range(8), next_one + next_stress)
        two = velocity(two, minus(edge(two), rim), vel, lane)
        add(b, 0, range(8), two)

        one = velocity_share([up[i, mine, :] for i in range(3)], vel)
        met = [(high[i, mine, :] + v) * has_high for i, v in enumerate(front(one))]
        own_stress = side_share(met, coeffs)
        poro = poro + own_stress[3] * seen(b, 2, last)
        two = one + stress_share(one, [-v for v in front(one)], coeffs, lane)
        full = plus([up[3 + i, mine, :] for i in range(3)], [own_stress[0], own_stress[2], own_stress[3]])
        two = velocity(two, minus(edge(two), full), vel, lane)
        beyond = [v * has_high for v in front(two)]
        own = velocity([zero] * 4 + own_stress, [own_stress[0], own_stress[2], own_stress[3]], vel, lane)
        perm = perm + own[QX] * seen(b, 3, last) + own[QZ] * seen(b, 4, last)
        prior = side_share(front(own), coeffs)
        own = stress(own, minus(beyond, front(own)), coeffs, lane)
        poro = poro + own[PR] * seen(b, 5, last) + prior[3] * seen(b, 5, last - 1)
        add(b, last, range(8), own)
        add(b, last - 1, range(XX, 8), prior)

    pl.when(me > 0)(ups[1].wait_recv)
    pl.when(me < n - 1)(downs[1].wait_recv)
    for b in blocks:
        mine = own_block(b)
        late = velocity_share([low[3 + i, mine, :] for i in range(3)], vel)
        two = [keep[slot_of[0] + f, mine, :] for f in range(8)]
        two = plus(two[:4], late) + two[4:]
        perm = perm + two[QX] * seen(b, 3, 0) + two[QZ] * seen(b, 4, 0)
        after = [keep[slot_of[1] + f, mine, :] for f in (VX, VZ, QX)]
        two = stress(two, minus(after, front(two)), coeffs, lane)
        poro = poro + two[PR] * seen(b, 5, 0)
        add(b, 0, range(8), two)
        poro = poro - high[3, mine, :] * seen(b, 5, last)

    totals = (perm, poro)
    sums[me] = jnp.concatenate([jnp.sum(total, axis=0, keepdims=True) for total in totals], axis=0)

    @pl.when(me < n - 1)
    def _():
        pl.semaphore_wait(here, n - 1 - me)

    def send(peer, _):
        @pl.when(peer != me)
        def _():
            pltpu.make_async_remote_copy(
                sums.at[me], sums.at[me], sum_send, sum_recv,
                device_id={"gx": peer}, device_id_type=pl.DeviceIdType.MESH,
            ).start()

    lax.fori_loop(0, n, send, None)
    pl.when(me < n - 1)(downs[2].wait_recv)
    for b in blocks:
        mine = own_block(b)
        beyond_x, beyond_z = high[4, mine, :], high[5, mine, :]
        beyond_flow = (high[3, mine, :] - coeffs[2] * beyond_x) / coeffs[3]
        late = side_share([beyond_x, beyond_z, beyond_flow], coeffs)[:3] + [-high[3, mine, :]]
        add(b, last, range(XX, 8), plus([keep[slot_of[last] + f, mine, :] for f in range(XX, 8)], late))
    for b in blocks:
        for x in (0, 1, last, last - 1):
            at = pl.ds(b * 8 * rows + x, 8, stride=rows)
            for f in range(XX if x == last - 1 else 0, 8):
                out_ref[f, at, :] = out_ref[f, at, :] + keep[slot_of[x] + f, b * 8 : (b + 1) * 8, :]
    pltpu.make_async_copy(sums.at[pl.ds(1, n - 1)], sums.at[pl.ds(0, n - 1)], sum_recv).wait()
    sums_ref[...] = sums[...]
    pltpu.make_async_copy(sums.at[pl.ds(1, n - 1)], sums.at[pl.ds(0, n - 1)], sum_send).wait()
    for copy in ups:
        pl.when(me < n - 1)(copy.wait_send)
    for copy in downs:
        pl.when(me > 0)(copy.wait_send)


def write(out_ref, sums_ref, factor_ref, out_hbm, grad_hbm, grad, sems):
    half = out_ref.shape[0] // 2
    parts = [pl.ds(0, half), pl.ds(half, half)]
    copies = [pltpu.make_async_copy(out_ref.at[at], out_hbm.at[at], sems.at[i]) for i, at in enumerate(parts)]
    for copy in copies:
        copy.start()
    grad[...] = factor_ref[...] * jnp.sum(sums_ref[...], axis=0)
    copies.append(pltpu.make_async_copy(grad, grad_hbm, sems.at[2]))
    copies[2].start()
    for copy in copies:
        copy.wait()


def shards(adjoint_state, forward_fields, vel_coeffs, stress_coeffs, drm_cells, drm_force, source_id):
    fields, events, rows, depth = adjoint_state.shape
    cells = events * rows
    n = lax.axis_size("gx")
    scale = (events * rows * n) ** (-0.5)
    hbm, vmem = pl.BlockSpec(memory_space=pltpu.HBM), pl.BlockSpec(memory_space=pltpu.VMEM)
    f32 = jnp.float32
    dma = pltpu.SemaphoreType.DMA
    out, sums, factor = pl.pallas_call(
        functools.partial(kernel, n, scale),
        out_shape=[
            pltpu.VMEM((fields, cells, depth), f32),
            pltpu.VMEM((n, 2, depth), f32),
            pltpu.VMEM((2, depth), f32),
        ],
        in_specs=[hbm] * 7,
        out_specs=[vmem] * 3,
        scratch_shapes=[
            pltpu.VMEM((fields, cells, depth), f32),
            pltpu.VMEM((6, cells, depth), jnp.bfloat16),
            pltpu.VMEM(vel_coeffs.shape, f32),
            pltpu.VMEM(stress_coeffs.shape, f32),
            pltpu.VMEM((1, drm_cells.shape[0]), jnp.int32),
            pltpu.VMEM(drm_force.shape, f32),
            pltpu.SMEM(source_id.shape, jnp.int32),
            pltpu.VMEM((4 * drm_force.shape[0] * rows, depth), f32),
            pltpu.VMEM((4 * drm_force.shape[0], rows, depth), f32),
            pltpu.VMEM((6, cells, depth), f32),
            pltpu.VMEM((32, events, depth), f32),
            pltpu.VMEM((6, events, depth), f32),
            pltpu.VMEM((6, events, depth), f32),
            pltpu.VMEM((6, events, depth), f32),
            pltpu.VMEM((6, events, depth), f32),
            pltpu.VMEM((n, 2, depth), f32),
            dma((3,)),
            dma,
            dma((5,)),
            dma((2, 2)),
            dma((2, 3)),
            dma,
            dma,
            pltpu.SemaphoreType.REGULAR,
        ],
        compiler_params=pltpu.CompilerParams(
            collective_id=0, has_side_effects=True
        ),
    )(
        adjoint_state.reshape(fields, cells, depth),
        forward_fields.reshape(6, cells, depth),
        vel_coeffs,
        stress_coeffs,
        drm_cells.reshape(1, -1),
        drm_force,
        source_id,
    )
    held = [pltpu.with_memory_space_constraint(v, pltpu.VMEM) for v in (out, sums, factor)]
    out, gradients = pl.pallas_call(
        write,
        out_shape=[jax.ShapeDtypeStruct(out.shape, f32), jax.ShapeDtypeStruct(vel_coeffs[:2].shape, f32)],
        in_specs=[pl.BlockSpec(memory_space=pl.ANY), vmem, vmem],
        out_specs=[hbm, hbm],
        scratch_shapes=[pltpu.VMEM((2, depth), f32), dma((3,))],
    )(*held)
    return out.reshape(adjoint_state.shape), gradients


def solution(mesh):
    in_specs = (
        P(None, "groups", "gx", None),
        P(None, None, "groups", "gx", None),
        P("groups", None),
        P("groups", None),
        P("gx"),
        P("groups", None, None, "gx"),
        P("groups"),
    )
    out_specs = (P(None, "groups", "gx", None), P("groups", None))
    return jax.shard_map(shards, mesh=mesh, in_specs=in_specs, out_specs=out_specs, check_vma=False)
```

```python
import functools

import jax
import jax.numpy as jnp
from jax import lax
from jax.experimental import pallas as pl
from jax.experimental.pallas import tpu as pltpu
from jax.sharding import PartitionSpec as P

LAYER = 8
VX, VZ, QX, QZ, XX, ZZ, XZ, PR = range(8)


def coeff_rows(coeffs):
    return [coeffs[i : i + 1] for i in range(4)]


def depth_lower(values, lane):
    return values - jnp.where(lane == 0, 0.0, pltpu.roll(values, 1, 1))


def depth_upper(values, lane):
    last = values.shape[1] - 1
    return jnp.where(lane == last, 0.0, pltpu.roll(values, last, 1)) - values


def velocity(fields, sides, vel, lane, forcing=None):
    vel_x, vel_z, flow_x, flow_z, _, stress_zz, stress_xz, pressure = fields
    solid, couple, fluid, drag = vel
    force_x = sides[0] + depth_lower(stress_xz, lane)
    force_z = sides[1] + depth_lower(stress_zz, lane)
    push_x = sides[2] + drag * flow_x
    push_z = depth_lower(pressure, lane) + drag * flow_z
    new_x = vel_x + solid * force_x + couple * push_x
    new_z = vel_z + solid * force_z + couple * push_z
    if forcing is not None:
        new_x = new_x + forcing[0]
        new_z = new_z + forcing[1]
    flow_x = flow_x - couple * force_x - fluid * push_x
    flow_z = flow_z - couple * force_z - fluid * push_z
    return [new_x, new_z, flow_x, flow_z, *fields[4:]]


def stress(fields, sides, coeffs, lane):
    vel_x, vel_z, flow_x, flow_z, xx, zz, xz, pressure = fields
    lame, shear, couple, fluid = coeffs
    strain_z = depth_upper(vel_z, lane)
    dilation = sides[0] + strain_z
    inflow = sides[2] + depth_upper(flow_z, lane)
    shared = lame * dilation - couple * inflow
    twice = 2.0 * shear
    xx = xx + shared + twice * sides[0]
    zz = zz + shared + twice * strain_z
    xz = xz + shear * (depth_upper(vel_x, lane) + sides[1])
    pressure = pressure - couple * dilation - fluid * inflow
    return [vel_x, vel_z, flow_x, flow_z, xx, zz, xz, pressure]


def side_share(row, coeffs):
    lame, shear, couple, fluid = coeffs
    zz = lame * row[0] - couple * row[2]
    pressure = -couple * row[0] - fluid * row[2]
    return [zz + 2.0 * shear * row[0], zz, shear * row[1], pressure]


def beyond_share(row, coeffs):
    xx, _, xz, pressure = side_share(row, coeffs)
    return [xx, xz, pressure]


def velocity_share(row, vel):
    solid, couple, fluid, _ = vel
    xx, xz, pressure = row
    return [-(solid * xx + couple * pressure), -solid * xz, couple * xx + fluid * pressure, couple * xz]


def velocity_stress(pulled, vel, lane):
    solid, couple, fluid, _ = vel
    xx, zz, xz, pressure = pulled
    force_x = xx + depth_lower(xz, lane)
    force_z = xz + depth_lower(zz, lane)
    push_z = depth_lower(pressure, lane)
    return [
        solid * force_x + couple * pressure,
        solid * force_z + couple * push_z,
        -couple * force_x - fluid * pressure,
        -couple * force_z - fluid * push_z,
    ]


def stress_share(moved, sides, coeffs, lane):
    vel_x, vel_z, flow_x, flow_z = moved
    lame, shear, couple, fluid = coeffs
    strain_z = depth_upper(vel_z, lane)
    dilation = sides[0] + strain_z
    inflow = sides[2] + depth_upper(flow_z, lane)
    shared = lame * dilation - couple * inflow
    twice = 2.0 * shear
    return [
        shared + twice * sides[0],
        shared + twice * strain_z,
        shear * (depth_upper(vel_x, lane) + sides[1]),
        -couple * dilation - fluid * inflow,
    ]


def edge(fields):
    return [fields[XX], fields[XZ], fields[PR]]


def front(fields):
    return [fields[VX], fields[VZ], fields[QX]]


def minus(first, second):
    return [a - b for a, b in zip(first, second)]


def plus(first, second):
    return [a + b for a, b in zip(first, second)]


def kernel(
    n, scale, st_hbm, fw_hbm, vc_hbm, sc_hbm, cell_hbm, df_hbm, sid_hbm, out_ref, sums_ref, factor_ref,
    st, fw, vc_ref, sc_ref, cell_ref, df_ref, sid_ref, flat, tab, wide, keep, up, down, low, high, sums,
    st_sem, fw_sem, small_sem, up_sem, down_sem, sum_send, sum_recv, here,
):
    _, cells, depth = st.shape
    events = up.shape[1]
    rows = cells // events
    sources = df_ref.shape[0]
    me = lax.axis_index("gx")
    barrier = pltpu.get_barrier_semaphore()

    def greet(semaphore, peer):
        pl.semaphore_signal(semaphore, inc=1, device_id={"gx": peer}, device_id_type=pl.DeviceIdType.MESH)

    @pl.when(me > 0)
    def _():
        greet(barrier, me - 1)

    @pl.when(me < n - 1)
    def _():
        greet(barrier, me + 1)

    smalls = [
        pltpu.make_async_copy(src, dst, small_sem.at[i])
        for i, (src, dst) in enumerate(
            [(df_hbm, df_ref), (cell_hbm, cell_ref), (sid_hbm, sid_ref), (vc_hbm, vc_ref), (sc_hbm, sc_ref)]
        )
    ]
    for small in smalls:
        small.start()
    last = rows - 1
    from_hbm, to_vmem = st_hbm.reshape(8, events, rows, depth), st.reshape(8, events, rows, depth)
    loads = [
        pltpu.make_async_copy(from_hbm.at[:, :, at], to_vmem.at[:, :, at], st_sem.at[i])
        for i, at in enumerate([pl.ds(0, 2), pl.ds(last - 1, 2), pl.ds(2, rows - 4)])
    ]
    loads[0].start()
    loads[1].start()
    fw_load = pltpu.make_async_copy(fw_hbm, fw, fw_sem)
    lax.fori_loop(me + 2, n, lambda peer, _: greet(barrier, peer), None)

    @pl.when(me == 0)
    def _():
        low[...] = jnp.zeros(low.shape, jnp.float32)

    @pl.when(me == n - 1)
    def _():
        high[...] = jnp.zeros(high.shape, jnp.float32)

    for small in smalls:
        small.wait()
    vel = coeff_rows(vc_ref[...])
    coeffs = coeff_rows(sc_ref[...])

    def three(values):
        first = values.astype(jnp.bfloat16)
        rest = values - first.astype(jnp.float32)
        second = rest.astype(jnp.bfloat16)
        return [first, second, (rest - second.astype(jnp.float32)).astype(jnp.bfloat16)]

    force = jnp.concatenate([df_ref[:, t, c, :] for t in range(2) for c in range(2)], axis=0)
    count = force.shape[0]
    place = cell_ref[...] - me * (rows * depth)
    column = lax.broadcasted_iota(jnp.int32, (depth, place.shape[1]), 0)
    spot = (column // LAYER) * depth + (depth - LAYER) + lax.rem(column, LAYER)
    hot = jnp.where(spot == place, 1.0, 0.0).astype(jnp.bfloat16)
    got = lax.dot_general(
        jnp.concatenate(three(force), axis=0), hot, (((1,), (1,)), ((), ())), preferred_element_type=jnp.float32
    )
    got = got[:count] + got[count : 2 * count] + got[2 * count :]

    def placed(values, x):
        at = lax.broadcasted_iota(jnp.int32, values.shape, 1)
        return jnp.where(at < depth - LAYER, 0.0, pltpu.roll(values, depth - LAYER - x * LAYER, 1))

    row_id = lax.broadcasted_iota(jnp.int32, (8, sources), 0)
    source_at = lax.broadcasted_iota(jnp.int32, (8, sources), 1)
    blocks = []
    for b in range(events // 8):
        wanted = jnp.full((8, sources), sid_ref[b * 8], jnp.int32)
        for r in range(1, 8):
            wanted = jnp.where(row_id == r, sid_ref[b * 8 + r], wanted)
        blocks.append(jnp.where(wanted == source_at, 1.0, 0.0))
    picked = jnp.concatenate(blocks, axis=0).astype(jnp.bfloat16)
    picked = jnp.concatenate([picked] * 3, axis=1)

    def event_forcing(t):
        return [
            jnp.dot(
                picked, jnp.concatenate(three(got[(t * 2 + c) * sources : (t * 2 + c + 1) * sources]), axis=0),
                preferred_element_type=jnp.float32,
            )
            for c in range(2)
        ]

    slot_of = {0: 0, 1: 8, last: 16, last - 1: 24}
    now, later = event_forcing(0), event_forcing(1)
    force_0, force_1, force_last = [[placed(v, x) for v in now] for x in (0, 1, last)]
    later_0 = [placed(v, 0) for v in later]

    lane = lax.broadcasted_iota(jnp.int32, (8, depth), 1)
    at_row = lax.broadcasted_iota(jnp.int32, (rows, depth), 0)
    zero = jnp.zeros((8, depth), jnp.float32)
    blocks = range(events // 8)

    ups, downs = [], []
    for c in range(2):
        half = pl.ds(3 * c, 3)
        ups.append(
            pltpu.make_async_remote_copy(
                up.at[half], low.at[half], up_sem.at[0, c], up_sem.at[1, c],
                device_id={"gx": jnp.minimum(me + 1, n - 1)}, device_id_type=pl.DeviceIdType.MESH,
            )
        )
    for c, part in enumerate([pl.ds(0, 3), pl.ds(3, 1), pl.ds(4, 2)]):
        downs.append(
            pltpu.make_async_remote_copy(
                down.at[part], high.at[part], down_sem.at[0, c], down_sem.at[1, c],
                device_id={"gx": jnp.maximum(me - 1, 0)}, device_id_type=pl.DeviceIdType.MESH,
            )
        )

    def own_block(b):
        return slice(b * 8, (b + 1) * 8)

    def row(b, x, names=range(8)):
        return [st[f, pl.ds(b * 8 * rows + x, 8, stride=rows), :] for f in names]

    loads[0].wait()
    loads[2].start()
    fw_load.start()
    firsts = []
    for b in blocks:
        row_0 = row(b, 0)
        one_0 = velocity(row_0, edge(row_0), vel, lane, [v[own_block(b)] for v in force_0])
        for i, v in enumerate(front(one_0)):
            down[i, own_block(b), :] = v
        firsts.append(one_0)
    pl.semaphore_wait(barrier, me + jnp.where(me < n - 1, 1, 0))
    pl.when(me > 0)(downs[0].start)
    loads[1].wait()
    for b in blocks:
        for i, v in enumerate(row(b, last, (XX, XZ, PR))):
            up[i, own_block(b), :] = v
    pl.when(me < n - 1)(ups[0].start)
    for b in blocks:
        mine = own_block(b)
        row_0, row_1, one_0 = row(b, 0, (XX, XZ, PR)), row(b, 1), firsts[b]
        one_1 = velocity(row_1, minus(edge(row_1), row_0), vel, lane, [v[mine] for v in force_1])
        two_0 = stress(one_0, minus(front(one_1), front(one_0)), coeffs, lane)
        two_0 = velocity(two_0, edge(two_0), vel, lane, [v[mine] for v in later_0])
        down[3, mine, :] = coeffs[2] * two_0[VX] + coeffs[3] * two_0[QX]
        down[4, mine, :] = two_0[VX]
        down[5, mine, :] = two_0[VZ]
    pl.when(me > 0)(downs[1].start)
    for b in blocks:
        mine = own_block(b)
        row_last = row(b, last)
        sides = minus(edge(row_last), row(b, last - 1, (XX, XZ, PR)))
        one_last = velocity(row_last, sides, vel, lane, [v[mine] for v in force_last])
        one_last = stress(one_last, [-v for v in front(one_last)], coeffs, lane)
        for i, v in enumerate(edge(one_last)):
            up[3 + i, mine, :] = v
    pl.when(me < n - 1)(ups[1].start)

    for x in range(rows):
        flat[pl.ds(x, count, stride=rows), :] = placed(got, x)
    tab[...] = flat[...].reshape(tab.shape)
    loads[2].wait()
    lax.fori_loop(0, me, lambda peer, _: greet(here, peer), None)
    fw_load.wait()
    factor_ref[0:1, :] = vel[2] * vel[3] * scale
    factor_ref[1:2, :] = coeffs[3] * scale

    def lower(values):
        return values - jnp.where(at_row == 0, 0.0, pltpu.roll(values, 1, 0))

    def upper(values):
        return jnp.where(at_row == last, 0.0, pltpu.roll(values, last, 0)) - values

    def pair(i, totals):
        perm, poro = totals
        both = pl.ds(pl.multiple_of(i * 2 * rows, 2 * rows), 2 * rows)
        stored = [fw[k, both, :].astype(jnp.float32) for k in range(6)]
        for k in range(6):
            wide[k, both, :] = stored[k]
        for half in range(2):
            e = i * 2 + half
            at = pl.ds(pl.multiple_of(e * rows, rows), rows)
            own = slice(half * rows, (half + 1) * rows)
            source = sid_ref[e]
            fields = [st[f, at, :] for f in range(8)]
            for t in range(2):
                forcing = [tab[(t * 2 + c) * sources + source] for c in range(2)]
                fields = velocity(fields, [lower(v) for v in edge(fields)], vel, lane, forcing)
                perm = perm + fields[QX] * stored[3 * t][own] + fields[QZ] * stored[3 * t + 1][own]
                fields = stress(fields, [upper(v) for v in front(fields)], coeffs, lane)
                poro = poro + fields[PR] * stored[3 * t + 2][own]
            for f in range(8):
                out_ref[f, at, :] = fields[f]
        return perm, poro

    perm, poro = lax.fori_loop(0, events // 2, pair, (zero, zero), unroll=12)

    pl.when(me > 0)(downs[2].start)
    has_low = jnp.where(me > 0, 1.0, 0.0)
    has_high = jnp.where(me < n - 1, 1.0, 0.0)

    def seen(b, k, x):
        return wide[k, pl.ds(b * 8 * rows + x, 8, stride=rows), :]

    def add(b, x, names, values):
        for f, v in zip(names, values):
            keep[slot_of[x] + f, own_block(b), :] = v

    def sides_of(pulled):
        return [pulled[0], pulled[2], pulled[3]]

    def top(b, pulled, beyond, totals):
        perm, poro = totals
        moved = velocity_stress(pulled, vel, lane)
        perm = perm + moved[QX] * seen(b, 3, last) + moved[QZ] * seen(b, 4, last)
        prior = side_share(front(moved), coeffs)
        change = plus(pulled, stress_share(moved, minus(beyond, front(moved)), coeffs, lane))
        poro = poro + pulled[3] * seen(b, 2, last) + change[3] * seen(b, 5, last) + prior[3] * seen(b, 5, last - 1)
        return moved + change, prior, (perm, poro)

    pl.when(me > 0)(ups[0].wait_recv)
    for b in blocks:
        mine = own_block(b)
        one = velocity_share([low[i, mine, :] for i in range(3)], vel)
        perm = perm + one[QX] * seen(b, 0, 0) + one[QZ] * seen(b, 1, 0)
        met = plus([down[i, mine, :] for i in range(3)], front(one))
        rim = [v * has_low for v in beyond_share(met, coeffs)]
        two = one + stress_share(one, [-v for v in front(one)], coeffs, lane)
        poro = poro + two[PR] * seen(b, 2, 0)
        next_one = velocity_share(edge(two), vel)
        perm = perm + next_one[QX] * seen(b, 3, 1) + next_one[QZ] * seen(b, 4, 1)
        next_stress = stress_share(next_one, [-v for v in front(next_one)], coeffs, lane)
        poro = poro + next_stress[3] * seen(b, 5, 1)
        add(b, 1, range(8), next_one + next_stress)
        two = velocity(two, minus(edge(two), rim), vel, lane)
        add(b, 0, range(8), two)

        one = velocity_share([up[i, mine, :] for i in range(3)], vel)
        pulled = [v * has_high for v in side_share(front(one), coeffs)]
        two = one + stress_share(one, [-v for v in front(one)], coeffs, lane)
        full = plus([up[3 + i, mine, :] for i in range(3)], sides_of(pulled))
        beyond = [v * has_high for v in front(velocity(two, minus(edge(two), full), vel, lane))]
        own, prior, (perm, poro) = top(b, pulled, beyond, (perm, poro))
        add(b, last, range(8), own)
        add(b, last - 1, range(XX, 8), prior)

    pl.when(me < n - 1)(downs[0].wait_recv)
    for b in blocks:
        pulled = side_share([high[i, own_block(b), :] for i in range(3)], coeffs)
        beyond = front(velocity_share(sides_of(pulled), vel))
        own, prior, (perm, poro) = top(b, pulled, beyond, (perm, poro))
        add(b, last, range(8), plus(own, [keep[slot_of[last] + f, own_block(b), :] for f in range(8)]))
        more = [keep[slot_of[last - 1] + f, own_block(b), :] for f in range(XX, 8)]
        add(b, last - 1, range(XX, 8), plus(prior, more))

    pl.when(me > 0)(ups[1].wait_recv)
    for b in blocks:
        mine = own_block(b)
        late = velocity_share([low[3 + i, mine, :] for i in range(3)], vel)
        two = [keep[slot_of[0] + f, mine, :] for f in range(8)]
        two = plus(two[:4], late) + two[4:]
        perm = perm + two[QX] * seen(b, 3, 0) + two[QZ] * seen(b, 4, 0)
        after = [keep[slot_of[1] + f, mine, :] for f in (VX, VZ, QX)]
        two = stress(two, minus(after, front(two)), coeffs, lane)
        poro = poro + two[PR] * seen(b, 5, 0)
        add(b, 0, range(8), two)

    pl.when(me < n - 1)(downs[1].wait_recv)
    for b in blocks:
        poro = poro - high[3, own_block(b), :] * seen(b, 5, last)

    totals = (perm, poro)
    sums[me] = jnp.concatenate([jnp.sum(total, axis=0, keepdims=True) for total in totals], axis=0)

    @pl.when(me < n - 1)
    def _():
        pl.semaphore_wait(here, n - 1 - me)

    def send(peer, _):
        @pl.when(peer != me)
        def _():
            pltpu.make_async_remote_copy(
                sums.at[me], sums.at[me], sum_send, sum_recv,
                device_id={"gx": peer}, device_id_type=pl.DeviceIdType.MESH,
            ).start()

    lax.fori_loop(0, n, send, None)
    pl.when(me < n - 1)(downs[2].wait_recv)
    for b in blocks:
        mine = own_block(b)
        beyond_x, beyond_z = high[4, mine, :], high[5, mine, :]
        beyond_flow = (high[3, mine, :] - coeffs[2] * beyond_x) / coeffs[3]
        late = side_share([beyond_x, beyond_z, beyond_flow], coeffs)[:3] + [-high[3, mine, :]]
        add(b, last, range(XX, 8), plus([keep[slot_of[last] + f, mine, :] for f in range(XX, 8)], late))
    for b in blocks:
        for x in (0, 1, last, last - 1):
            at = pl.ds(b * 8 * rows + x, 8, stride=rows)
            for f in range(XX if x == last - 1 else 0, 8):
                out_ref[f, at, :] = out_ref[f, at, :] + keep[slot_of[x] + f, b * 8 : (b + 1) * 8, :]
    pltpu.make_async_copy(sums.at[pl.ds(1, n - 1)], sums.at[pl.ds(0, n - 1)], sum_recv).wait()
    sums_ref[...] = sums[...]
    pltpu.make_async_copy(sums.at[pl.ds(1, n - 1)], sums.at[pl.ds(0, n - 1)], sum_send).wait()
    for copy in ups:
        pl.when(me < n - 1)(copy.wait_send)
    for copy in downs:
        pl.when(me > 0)(copy.wait_send)


def write(out_ref, sums_ref, factor_ref, out_hbm, grad_hbm, grad, sems):
    half = out_ref.shape[0] // 2
    parts = [pl.ds(0, half), pl.ds(half, half)]
    copies = [pltpu.make_async_copy(out_ref.at[at], out_hbm.at[at], sems.at[i]) for i, at in enumerate(parts)]
    for copy in copies:
        copy.start()
    grad[...] = factor_ref[...] * jnp.sum(sums_ref[...], axis=0)
    copies.append(pltpu.make_async_copy(grad, grad_hbm, sems.at[2]))
    copies[2].start()
    for copy in copies:
        copy.wait()


def shards(adjoint_state, forward_fields, vel_coeffs, stress_coeffs, drm_cells, drm_force, source_id):
    fields, events, rows, depth = adjoint_state.shape
    cells = events * rows
    n = lax.axis_size("gx")
    scale = (events * rows * n) ** (-0.5)
    hbm, vmem = pl.BlockSpec(memory_space=pltpu.HBM), pl.BlockSpec(memory_space=pltpu.VMEM)
    f32 = jnp.float32
    dma = pltpu.SemaphoreType.DMA
    out, sums, factor = pl.pallas_call(
        functools.partial(kernel, n, scale),
        out_shape=[
            pltpu.VMEM((fields, cells, depth), f32),
            pltpu.VMEM((n, 2, depth), f32),
            pltpu.VMEM((2, depth), f32),
        ],
        in_specs=[hbm] * 7,
        out_specs=[vmem] * 3,
        scratch_shapes=[
            pltpu.VMEM((fields, cells, depth), f32),
            pltpu.VMEM((6, cells, depth), jnp.bfloat16),
            pltpu.VMEM(vel_coeffs.shape, f32),
            pltpu.VMEM(stress_coeffs.shape, f32),
            pltpu.VMEM((1, drm_cells.shape[0]), jnp.int32),
            pltpu.VMEM(drm_force.shape, f32),
            pltpu.SMEM(source_id.shape, jnp.int32),
            pltpu.VMEM((4 * drm_force.shape[0] * rows, depth), f32),
            pltpu.VMEM((4 * drm_force.shape[0], rows, depth), f32),
            pltpu.VMEM((6, cells, depth), f32),
            pltpu.VMEM((32, events, depth), f32),
            pltpu.VMEM((6, events, depth), f32),
            pltpu.VMEM((6, events, depth), f32),
            pltpu.VMEM((6, events, depth), f32),
            pltpu.VMEM((6, events, depth), f32),
            pltpu.VMEM((n, 2, depth), f32),
            dma((3,)),
            dma,
            dma((5,)),
            dma((2, 2)),
            dma((2, 3)),
            dma,
            dma,
            pltpu.SemaphoreType.REGULAR,
        ],
        compiler_params=pltpu.CompilerParams(
            collective_id=0, has_side_effects=True
        ),
    )(
        adjoint_state.reshape(fields, cells, depth),
        forward_fields.reshape(6, cells, depth),
        vel_coeffs,
        stress_coeffs,
        drm_cells.reshape(1, -1),
        drm_force,
        source_id,
    )
    held = [pltpu.with_memory_space_constraint(v, pltpu.VMEM) for v in (out, sums, factor)]
    out, gradients = pl.pallas_call(
        write,
        out_shape=[jax.ShapeDtypeStruct(out.shape, f32), jax.ShapeDtypeStruct(vel_coeffs[:2].shape, f32)],
        in_specs=[pl.BlockSpec(memory_space=pl.ANY), vmem, vmem],
        out_specs=[hbm, hbm],
        scratch_shapes=[pltpu.VMEM((2, depth), f32), dma((3,))],
    )(*held)
    return out.reshape(adjoint_state.shape), gradients


def solution(mesh):
    in_specs = (
        P(None, "groups", "gx", None),
        P(None, None, "groups", "gx", None),
        P("groups", None),
        P("groups", None),
        P("gx"),
        P("groups", None, None, "gx"),
        P("groups"),
    )
    out_specs = (P(None, "groups", "gx", None), P("groups", None))
    return jax.shard_map(shards, mesh=mesh, in_specs=in_specs, out_specs=out_specs, check_vma=False)
```

```python
import functools

import jax
import jax.numpy as jnp
from jax import lax
from jax.experimental import pallas as pl
from jax.experimental.pallas import tpu as pltpu
from jax.sharding import PartitionSpec as P

LAYER = 8
VX, VZ, QX, QZ, XX, ZZ, XZ, PR = range(8)


def coeff_rows(coeffs):
    return [coeffs[i : i + 1] for i in range(4)]


def depth_lower(values, lane):
    return values - jnp.where(lane == 0, 0.0, pltpu.roll(values, 1, 1))


def depth_upper(values, lane):
    last = values.shape[1] - 1
    return jnp.where(lane == last, 0.0, pltpu.roll(values, last, 1)) - values


def velocity(fields, sides, vel, lane, forcing=None):
    vel_x, vel_z, flow_x, flow_z, _, stress_zz, stress_xz, pressure = fields
    solid, couple, fluid, drag = vel
    force_x = sides[0] + depth_lower(stress_xz, lane)
    force_z = sides[1] + depth_lower(stress_zz, lane)
    push_x = sides[2] + drag * flow_x
    push_z = depth_lower(pressure, lane) + drag * flow_z
    new_x = vel_x + solid * force_x + couple * push_x
    new_z = vel_z + solid * force_z + couple * push_z
    if forcing is not None:
        new_x = new_x + forcing[0]
        new_z = new_z + forcing[1]
    flow_x = flow_x - couple * force_x - fluid * push_x
    flow_z = flow_z - couple * force_z - fluid * push_z
    return [new_x, new_z, flow_x, flow_z, *fields[4:]]


def stress(fields, sides, coeffs, lane):
    vel_x, vel_z, flow_x, flow_z, xx, zz, xz, pressure = fields
    lame, shear, couple, fluid = coeffs
    strain_z = depth_upper(vel_z, lane)
    dilation = sides[0] + strain_z
    inflow = sides[2] + depth_upper(flow_z, lane)
    shared = lame * dilation - couple * inflow
    twice = 2.0 * shear
    xx = xx + shared + twice * sides[0]
    zz = zz + shared + twice * strain_z
    xz = xz + shear * (depth_upper(vel_x, lane) + sides[1])
    pressure = pressure - couple * dilation - fluid * inflow
    return [vel_x, vel_z, flow_x, flow_z, xx, zz, xz, pressure]


def side_share(row, coeffs):
    lame, shear, couple, fluid = coeffs
    zz = lame * row[0] - couple * row[2]
    pressure = -couple * row[0] - fluid * row[2]
    return [zz + 2.0 * shear * row[0], zz, shear * row[1], pressure]


def beyond_share(row, coeffs):
    xx, _, xz, pressure = side_share(row, coeffs)
    return [xx, xz, pressure]


def velocity_share(row, vel):
    solid, couple, fluid, _ = vel
    xx, xz, pressure = row
    return [-(solid * xx + couple * pressure), -solid * xz, couple * xx + fluid * pressure, couple * xz]


def velocity_stress(pulled, vel, lane):
    solid, couple, fluid, _ = vel
    xx, zz, xz, pressure = pulled
    force_x = xx + depth_lower(xz, lane)
    force_z = xz + depth_lower(zz, lane)
    push_z = depth_lower(pressure, lane)
    return [
        solid * force_x + couple * pressure,
        solid * force_z + couple * push_z,
        -couple * force_x - fluid * pressure,
        -couple * force_z - fluid * push_z,
    ]


def stress_share(moved, sides, coeffs, lane):
    vel_x, vel_z, flow_x, flow_z = moved
    lame, shear, couple, fluid = coeffs
    strain_z = depth_upper(vel_z, lane)
    dilation = sides[0] + strain_z
    inflow = sides[2] + depth_upper(flow_z, lane)
    shared = lame * dilation - couple * inflow
    twice = 2.0 * shear
    return [
        shared + twice * sides[0],
        shared + twice * strain_z,
        shear * (depth_upper(vel_x, lane) + sides[1]),
        -couple * dilation - fluid * inflow,
    ]


def edge(fields):
    return [fields[XX], fields[XZ], fields[PR]]


def front(fields):
    return [fields[VX], fields[VZ], fields[QX]]


def minus(first, second):
    return [a - b for a, b in zip(first, second)]


def plus(first, second):
    return [a + b for a, b in zip(first, second)]


def kernel(
    n, scale, st_hbm, fw_hbm, vc_hbm, sc_hbm, cell_hbm, df_hbm, sid_hbm, out_ref, sums_ref, factor_ref,
    st, fw, vc_ref, sc_ref, cell_ref, df_ref, sid_ref, flat, tab, wide, keep, up, down, low, high, sums,
    st_sem, fw_sem, small_sem, up_sem, down_sem, sum_send, sum_recv, here,
):
    _, cells, depth = st.shape
    events = up.shape[1]
    rows = cells // events
    sources = df_ref.shape[0]
    me = lax.axis_index("gx")
    barrier = pltpu.get_barrier_semaphore()

    def greet(semaphore, peer):
        pl.semaphore_signal(semaphore, inc=1, device_id={"gx": peer}, device_id_type=pl.DeviceIdType.MESH)

    @pl.when(me > 0)
    def _():
        greet(barrier, me - 1)

    @pl.when(me < n - 1)
    def _():
        greet(barrier, me + 1)

    smalls = [
        pltpu.make_async_copy(src, dst, small_sem.at[i])
        for i, (src, dst) in enumerate(
            [(df_hbm, df_ref), (cell_hbm, cell_ref), (sid_hbm, sid_ref), (vc_hbm, vc_ref), (sc_hbm, sc_ref)]
        )
    ]
    for small in smalls:
        small.start()
    last = rows - 1
    from_hbm, to_vmem = st_hbm.reshape(8, events, rows, depth), st.reshape(8, events, rows, depth)
    loads = [
        pltpu.make_async_copy(from_hbm.at[:, :, at], to_vmem.at[:, :, at], st_sem.at[i])
        for i, at in enumerate([pl.ds(0, 2), pl.ds(last - 1, 2), pl.ds(2, rows - 4)])
    ]
    loads[0].start()
    loads[1].start()
    fw_load = pltpu.make_async_copy(fw_hbm, fw, fw_sem)
    lax.fori_loop(me + 2, n, lambda peer, _: greet(barrier, peer), None)

    @pl.when(me == 0)
    def _():
        low[...] = jnp.zeros(low.shape, jnp.float32)

    @pl.when(me == n - 1)
    def _():
        high[...] = jnp.zeros(high.shape, jnp.float32)

    for small in smalls:
        small.wait()
    vel = coeff_rows(vc_ref[...])
    coeffs = coeff_rows(sc_ref[...])

    def three(values):
        first = values.astype(jnp.bfloat16)
        rest = values - first.astype(jnp.float32)
        second = rest.astype(jnp.bfloat16)
        return [first, second, (rest - second.astype(jnp.float32)).astype(jnp.bfloat16)]

    force = jnp.concatenate([df_ref[:, t, c, :] for t in range(2) for c in range(2)], axis=0)
    count = force.shape[0]
    place = cell_ref[...] - me * (rows * depth)
    column = lax.broadcasted_iota(jnp.int32, (depth, place.shape[1]), 0)
    spot = (column // LAYER) * depth + (depth - LAYER) + lax.rem(column, LAYER)
    hot = jnp.where(spot == place, 1.0, 0.0).astype(jnp.bfloat16)
    got = lax.dot_general(
        jnp.concatenate(three(force), axis=0), hot, (((1,), (1,)), ((), ())), preferred_element_type=jnp.float32
    )
    got = got[:count] + got[count : 2 * count] + got[2 * count :]

    def placed(values, x):
        at = lax.broadcasted_iota(jnp.int32, values.shape, 1)
        return jnp.where(at < depth - LAYER, 0.0, pltpu.roll(values, depth - LAYER - x * LAYER, 1))

    row_id = lax.broadcasted_iota(jnp.int32, (8, sources), 0)
    source_at = lax.broadcasted_iota(jnp.int32, (8, sources), 1)
    blocks = []
    for b in range(events // 8):
        wanted = jnp.full((8, sources), sid_ref[b * 8], jnp.int32)
        for r in range(1, 8):
            wanted = jnp.where(row_id == r, sid_ref[b * 8 + r], wanted)
        blocks.append(jnp.where(wanted == source_at, 1.0, 0.0))
    picked = jnp.concatenate(blocks, axis=0).astype(jnp.bfloat16)
    picked = jnp.concatenate([picked] * 3, axis=1)

    def event_forcing(t):
        return [
            jnp.dot(
                picked, jnp.concatenate(three(got[(t * 2 + c) * sources : (t * 2 + c + 1) * sources]), axis=0),
                preferred_element_type=jnp.float32,
            )
            for c in range(2)
        ]

    slot_of = {0: 0, 1: 8, last: 16, last - 1: 24}
    now, later = event_forcing(0), event_forcing(1)
    force_0, force_1, force_last = [[placed(v, x) for v in now] for x in (0, 1, last)]
    later_0 = [placed(v, 0) for v in later]

    lane = lax.broadcasted_iota(jnp.int32, (8, depth), 1)
    at_row = lax.broadcasted_iota(jnp.int32, (rows, depth), 0)
    zero = jnp.zeros((8, depth), jnp.float32)
    blocks = range(events // 8)

    ups, downs = [], []
    for c in range(2):
        half = pl.ds(3 * c, 3)
        ups.append(
            pltpu.make_async_remote_copy(
                up.at[half], low.at[half], up_sem.at[0, c], up_sem.at[1, c],
                device_id={"gx": jnp.minimum(me + 1, n - 1)}, device_id_type=pl.DeviceIdType.MESH,
            )
        )
    for c, part in enumerate([pl.ds(0, 3), pl.ds(3, 1), pl.ds(4, 2)]):
        downs.append(
            pltpu.make_async_remote_copy(
                down.at[part], high.at[part], down_sem.at[0, c], down_sem.at[1, c],
                device_id={"gx": jnp.maximum(me - 1, 0)}, device_id_type=pl.DeviceIdType.MESH,
            )
        )

    def own_block(b):
        return slice(b * 8, (b + 1) * 8)

    def row(b, x, names=range(8)):
        return [st[f, pl.ds(b * 8 * rows + x, 8, stride=rows), :] for f in names]

    loads[0].wait()
    loads[2].start()
    fw_load.start()
    firsts = []
    for b in blocks:
        row_0 = row(b, 0)
        one_0 = velocity(row_0, edge(row_0), vel, lane, [v[own_block(b)] for v in force_0])
        for i, v in enumerate(front(one_0)):
            down[i, own_block(b), :] = v
        firsts.append(one_0)
    pl.semaphore_wait(barrier, me + jnp.where(me < n - 1, 1, 0))
    pl.when(me > 0)(downs[0].start)
    loads[1].wait()
    for b in blocks:
        for i, v in enumerate(row(b, last, (XX, XZ, PR))):
            up[i, own_block(b), :] = v
    pl.when(me < n - 1)(ups[0].start)
    for b in blocks:
        mine = own_block(b)
        row_0, row_1, one_0 = row(b, 0, (XX, XZ, PR)), row(b, 1), firsts[b]
        one_1 = velocity(row_1, minus(edge(row_1), row_0), vel, lane, [v[mine] for v in force_1])
        two_0 = stress(one_0, minus(front(one_1), front(one_0)), coeffs, lane)
        two_0 = velocity(two_0, edge(two_0), vel, lane, [v[mine] for v in later_0])
        down[3, mine, :] = coeffs[2] * two_0[VX] + coeffs[3] * two_0[QX]
        down[4, mine, :] = two_0[VX]
        down[5, mine, :] = two_0[VZ]
    pl.when(me > 0)(downs[1].start)
    for b in blocks:
        mine = own_block(b)
        row_last = row(b, last)
        sides = minus(edge(row_last), row(b, last - 1, (XX, XZ, PR)))
        one_last = velocity(row_last, sides, vel, lane, [v[mine] for v in force_last])
        one_last = stress(one_last, [-v for v in front(one_last)], coeffs, lane)
        for i, v in enumerate(edge(one_last)):
            up[3 + i, mine, :] = v
    pl.when(me < n - 1)(ups[1].start)

    for x in range(rows):
        flat[pl.ds(x, count, stride=rows), :] = placed(got, x)
    tab[...] = flat[...].reshape(tab.shape)
    loads[2].wait()
    lax.fori_loop(0, me, lambda peer, _: greet(here, peer), None)
    fw_load.wait()
    factor_ref[0:1, :] = vel[2] * vel[3] * scale
    factor_ref[1:2, :] = coeffs[3] * scale

    def lower(values):
        return values - jnp.where(at_row == 0, 0.0, pltpu.roll(values, 1, 0))

    def upper(values):
        return jnp.where(at_row == last, 0.0, pltpu.roll(values, last, 0)) - values

    def pair(i, totals):
        perm, poro = totals
        both = pl.ds(pl.multiple_of(i * 2 * rows, 2 * rows), 2 * rows)
        stored = [fw[k, both, :].astype(jnp.float32) for k in range(6)]
        for k in range(6):
            wide[k, both, :] = stored[k]
        for half in range(2):
            e = i * 2 + half
            at = pl.ds(pl.multiple_of(e * rows, rows), rows)
            own = slice(half * rows, (half + 1) * rows)
            source = sid_ref[e]
            fields = [st[f, at, :] for f in range(8)]
            for t in range(2):
                forcing = [tab[(t * 2 + c) * sources + source] for c in range(2)]
                fields = velocity(fields, [lower(v) for v in edge(fields)], vel, lane, forcing)
                perm = perm + fields[QX] * stored[3 * t][own] + fields[QZ] * stored[3 * t + 1][own]
                fields = stress(fields, [upper(v) for v in front(fields)], coeffs, lane)
                poro = poro + fields[PR] * stored[3 * t + 2][own]
            for f in range(8):
                out_ref[f, at, :] = fields[f]
        return perm, poro

    perm, poro = lax.fori_loop(0, events // 2, pair, (zero, zero), unroll=8)

    pl.when(me > 0)(downs[2].start)
    has_low = jnp.where(me > 0, 1.0, 0.0)
    has_high = jnp.where(me < n - 1, 1.0, 0.0)

    def seen(b, k, x):
        return wide[k, pl.ds(b * 8 * rows + x, 8, stride=rows), :]

    def add(b, x, names, values):
        for f, v in zip(names, values):
            keep[slot_of[x] + f, own_block(b), :] = v

    def sides_of(pulled):
        return [pulled[0], pulled[2], pulled[3]]

    def top(b, pulled, beyond, totals):
        perm, poro = totals
        moved = velocity_stress(pulled, vel, lane)
        perm = perm + moved[QX] * seen(b, 3, last) + moved[QZ] * seen(b, 4, last)
        prior = side_share(front(moved), coeffs)
        change = plus(pulled, stress_share(moved, minus(beyond, front(moved)), coeffs, lane))
        poro = poro + pulled[3] * seen(b, 2, last) + change[3] * seen(b, 5, last) + prior[3] * seen(b, 5, last - 1)
        return moved + change, prior, (perm, poro)

    pl.when(me > 0)(ups[0].wait_recv)
    for b in blocks:
        mine = own_block(b)
        one = velocity_share([low[i, mine, :] for i in range(3)], vel)
        perm = perm + one[QX] * seen(b, 0, 0) + one[QZ] * seen(b, 1, 0)
        met = plus([down[i, mine, :] for i in range(3)], front(one))
        rim = [v * has_low for v in beyond_share(met, coeffs)]
        two = one + stress_share(one, [-v for v in front(one)], coeffs, lane)
        poro = poro + two[PR] * seen(b, 2, 0)
        next_one = velocity_share(edge(two), vel)
        perm = perm + next_one[QX] * seen(b, 3, 1) + next_one[QZ] * seen(b, 4, 1)
        next_stress = stress_share(next_one, [-v for v in front(next_one)], coeffs, lane)
        poro = poro + next_stress[3] * seen(b, 5, 1)
        add(b, 1, range(8), next_one + next_stress)
        two = velocity(two, minus(edge(two), rim), vel, lane)
        add(b, 0, range(8), two)

        one = velocity_share([up[i, mine, :] for i in range(3)], vel)
        pulled = [v * has_high for v in side_share(front(one), coeffs)]
        two = one + stress_share(one, [-v for v in front(one)], coeffs, lane)
        full = plus([up[3 + i, mine, :] for i in range(3)], sides_of(pulled))
        beyond = [v * has_high for v in front(velocity(two, minus(edge(two), full), vel, lane))]
        own, prior, (perm, poro) = top(b, pulled, beyond, (perm, poro))
        add(b, last, range(8), own)
        add(b, last - 1, range(XX, 8), prior)

    pl.when(me < n - 1)(downs[0].wait_recv)
    for b in blocks:
        pulled = side_share([high[i, own_block(b), :] for i in range(3)], coeffs)
        beyond = front(velocity_share(sides_of(pulled), vel))
        own, prior, (perm, poro) = top(b, pulled, beyond, (perm, poro))
        add(b, last, range(8), plus(own, [keep[slot_of[last] + f, own_block(b), :] for f in range(8)]))
        more = [keep[slot_of[last - 1] + f, own_block(b), :] for f in range(XX, 8)]
        add(b, last - 1, range(XX, 8), plus(prior, more))

    pl.when(me > 0)(ups[1].wait_recv)
    for b in blocks:
        mine = own_block(b)
        late = velocity_share([low[3 + i, mine, :] for i in range(3)], vel)
        two = [keep[slot_of[0] + f, mine, :] for f in range(8)]
        two = plus(two[:4], late) + two[4:]
        perm = perm + two[QX] * seen(b, 3, 0) + two[QZ] * seen(b, 4, 0)
        after = [keep[slot_of[1] + f, mine, :] for f in (VX, VZ, QX)]
        two = stress(two, minus(after, front(two)), coeffs, lane)
        poro = poro + two[PR] * seen(b, 5, 0)
        add(b, 0, range(8), two)

    pl.when(me < n - 1)(downs[1].wait_recv)
    for b in blocks:
        poro = poro - high[3, own_block(b), :] * seen(b, 5, last)

    totals = (perm, poro)
    sums[me] = jnp.concatenate([jnp.sum(total, axis=0, keepdims=True) for total in totals], axis=0)

    @pl.when(me < n - 1)
    def _():
        pl.semaphore_wait(here, n - 1 - me)

    def send(peer, _):
        @pl.when(peer != me)
        def _():
            pltpu.make_async_remote_copy(
                sums.at[me], sums.at[me], sum_send, sum_recv,
                device_id={"gx": peer}, device_id_type=pl.DeviceIdType.MESH,
            ).start()

    lax.fori_loop(0, n, send, None)
    pl.when(me < n - 1)(downs[2].wait_recv)
    for b in blocks:
        mine = own_block(b)
        beyond_x, beyond_z = high[4, mine, :], high[5, mine, :]
        beyond_flow = (high[3, mine, :] - coeffs[2] * beyond_x) / coeffs[3]
        late = side_share([beyond_x, beyond_z, beyond_flow], coeffs)[:3] + [-high[3, mine, :]]
        add(b, last, range(XX, 8), plus([keep[slot_of[last] + f, mine, :] for f in range(XX, 8)], late))
    for b in blocks:
        for x in (0, 1, last, last - 1):
            at = pl.ds(b * 8 * rows + x, 8, stride=rows)
            for f in range(XX if x == last - 1 else 0, 8):
                out_ref[f, at, :] = out_ref[f, at, :] + keep[slot_of[x] + f, b * 8 : (b + 1) * 8, :]
    pltpu.make_async_copy(sums.at[pl.ds(1, n - 1)], sums.at[pl.ds(0, n - 1)], sum_recv).wait()
    sums_ref[...] = sums[...]
    pltpu.make_async_copy(sums.at[pl.ds(1, n - 1)], sums.at[pl.ds(0, n - 1)], sum_send).wait()
    for copy in ups:
        pl.when(me < n - 1)(copy.wait_send)
    for copy in downs:
        pl.when(me > 0)(copy.wait_send)


def write(out_ref, sums_ref, factor_ref, out_hbm, grad_hbm, grad, sems):
    half = out_ref.shape[0] // 2
    parts = [pl.ds(0, half), pl.ds(half, half)]
    copies = [pltpu.make_async_copy(out_ref.at[at], out_hbm.at[at], sems.at[i]) for i, at in enumerate(parts)]
    for copy in copies:
        copy.start()
    grad[...] = factor_ref[...] * jnp.sum(sums_ref[...], axis=0)
    copies.append(pltpu.make_async_copy(grad, grad_hbm, sems.at[2]))
    copies[2].start()
    for copy in copies:
        copy.wait()


def shards(adjoint_state, forward_fields, vel_coeffs, stress_coeffs, drm_cells, drm_force, source_id):
    fields, events, rows, depth = adjoint_state.shape
    cells = events * rows
    n = lax.axis_size("gx")
    scale = (events * rows * n) ** (-0.5)
    hbm, vmem = pl.BlockSpec(memory_space=pltpu.HBM), pl.BlockSpec(memory_space=pltpu.VMEM)
    f32 = jnp.float32
    dma = pltpu.SemaphoreType.DMA
    out, sums, factor = pl.pallas_call(
        functools.partial(kernel, n, scale),
        out_shape=[
            pltpu.VMEM((fields, cells, depth), f32),
            pltpu.VMEM((n, 2, depth), f32),
            pltpu.VMEM((2, depth), f32),
        ],
        in_specs=[hbm] * 7,
        out_specs=[vmem] * 3,
        scratch_shapes=[
            pltpu.VMEM((fields, cells, depth), f32),
            pltpu.VMEM((6, cells, depth), jnp.bfloat16),
            pltpu.VMEM(vel_coeffs.shape, f32),
            pltpu.VMEM(stress_coeffs.shape, f32),
            pltpu.VMEM((1, drm_cells.shape[0]), jnp.int32),
            pltpu.VMEM(drm_force.shape, f32),
            pltpu.SMEM(source_id.shape, jnp.int32),
            pltpu.VMEM((4 * drm_force.shape[0] * rows, depth), f32),
            pltpu.VMEM((4 * drm_force.shape[0], rows, depth), f32),
            pltpu.VMEM((6, cells, depth), f32),
            pltpu.VMEM((32, events, depth), f32),
            pltpu.VMEM((6, events, depth), f32),
            pltpu.VMEM((6, events, depth), f32),
            pltpu.VMEM((6, events, depth), f32),
            pltpu.VMEM((6, events, depth), f32),
            pltpu.VMEM((n, 2, depth), f32),
            dma((3,)),
            dma,
            dma((5,)),
            dma((2, 2)),
            dma((2, 3)),
            dma,
            dma,
            pltpu.SemaphoreType.REGULAR,
        ],
        compiler_params=pltpu.CompilerParams(
            collective_id=0, has_side_effects=True
        ),
    )(
        adjoint_state.reshape(fields, cells, depth),
        forward_fields.reshape(6, cells, depth),
        vel_coeffs,
        stress_coeffs,
        drm_cells.reshape(1, -1),
        drm_force,
        source_id,
    )
    held = [pltpu.with_memory_space_constraint(v, pltpu.VMEM) for v in (out, sums, factor)]
    out, gradients = pl.pallas_call(
        write,
        out_shape=[jax.ShapeDtypeStruct(out.shape, f32), jax.ShapeDtypeStruct(vel_coeffs[:2].shape, f32)],
        in_specs=[pl.BlockSpec(memory_space=pl.ANY), vmem, vmem],
        out_specs=[hbm, hbm],
        scratch_shapes=[pltpu.VMEM((2, depth), f32), dma((3,))],
    )(*held)
    return out.reshape(adjoint_state.shape), gradients


def solution(mesh):
    in_specs = (
        P(None, "groups", "gx", None),
        P(None, None, "groups", "gx", None),
        P("groups", None),
        P("groups", None),
        P("gx"),
        P("groups", None, None, "gx"),
        P("groups"),
    )
    out_specs = (P(None, "groups", "gx", None), P("groups", None))
    return jax.shard_map(shards, mesh=mesh, in_specs=in_specs, out_specs=out_specs, check_vma=False)
```

```python
import functools

import jax
import jax.numpy as jnp
from jax import lax
from jax.experimental import pallas as pl
from jax.experimental.pallas import tpu as pltpu
from jax.sharding import PartitionSpec as P

LAYER = 8
VX, VZ, QX, QZ, XX, ZZ, XZ, PR = range(8)


def coeff_rows(coeffs):
    return [coeffs[i : i + 1] for i in range(4)]


def depth_lower(values, lane):
    return values - jnp.where(lane == 0, 0.0, pltpu.roll(values, 1, 1))


def depth_upper(values, lane):
    last = values.shape[1] - 1
    return jnp.where(lane == last, 0.0, pltpu.roll(values, last, 1)) - values


def velocity(fields, sides, vel, lane, forcing=None):
    vel_x, vel_z, flow_x, flow_z, _, stress_zz, stress_xz, pressure = fields
    solid, couple, fluid, drag = vel
    force_x = sides[0] + depth_lower(stress_xz, lane)
    force_z = sides[1] + depth_lower(stress_zz, lane)
    push_x = sides[2] + drag * flow_x
    push_z = depth_lower(pressure, lane) + drag * flow_z
    new_x = vel_x + solid * force_x + couple * push_x
    new_z = vel_z + solid * force_z + couple * push_z
    if forcing is not None:
        new_x = new_x + forcing[0]
        new_z = new_z + forcing[1]
    flow_x = flow_x - couple * force_x - fluid * push_x
    flow_z = flow_z - couple * force_z - fluid * push_z
    return [new_x, new_z, flow_x, flow_z, *fields[4:]]


def stress(fields, sides, coeffs, lane):
    vel_x, vel_z, flow_x, flow_z, xx, zz, xz, pressure = fields
    lame, shear, couple, fluid = coeffs
    strain_z = depth_upper(vel_z, lane)
    dilation = sides[0] + strain_z
    inflow = sides[2] + depth_upper(flow_z, lane)
    shared = lame * dilation - couple * inflow
    twice = 2.0 * shear
    xx = xx + shared + twice * sides[0]
    zz = zz + shared + twice * strain_z
    xz = xz + shear * (depth_upper(vel_x, lane) + sides[1])
    pressure = pressure - couple * dilation - fluid * inflow
    return [vel_x, vel_z, flow_x, flow_z, xx, zz, xz, pressure]


def side_share(row, coeffs):
    lame, shear, couple, fluid = coeffs
    zz = lame * row[0] - couple * row[2]
    pressure = -couple * row[0] - fluid * row[2]
    return [zz + 2.0 * shear * row[0], zz, shear * row[1], pressure]


def beyond_share(row, coeffs):
    xx, _, xz, pressure = side_share(row, coeffs)
    return [xx, xz, pressure]


def velocity_share(row, vel):
    solid, couple, fluid, _ = vel
    xx, xz, pressure = row
    return [-(solid * xx + couple * pressure), -solid * xz, couple * xx + fluid * pressure, couple * xz]


def velocity_stress(pulled, vel, lane):
    solid, couple, fluid, _ = vel
    xx, zz, xz, pressure = pulled
    force_x = xx + depth_lower(xz, lane)
    force_z = xz + depth_lower(zz, lane)
    push_z = depth_lower(pressure, lane)
    return [
        solid * force_x + couple * pressure,
        solid * force_z + couple * push_z,
        -couple * force_x - fluid * pressure,
        -couple * force_z - fluid * push_z,
    ]


def stress_share(moved, sides, coeffs, lane):
    vel_x, vel_z, flow_x, flow_z = moved
    lame, shear, couple, fluid = coeffs
    strain_z = depth_upper(vel_z, lane)
    dilation = sides[0] + strain_z
    inflow = sides[2] + depth_upper(flow_z, lane)
    shared = lame * dilation - couple * inflow
    twice = 2.0 * shear
    return [
        shared + twice * sides[0],
        shared + twice * strain_z,
        shear * (depth_upper(vel_x, lane) + sides[1]),
        -couple * dilation - fluid * inflow,
    ]


def edge(fields):
    return [fields[XX], fields[XZ], fields[PR]]


def front(fields):
    return [fields[VX], fields[VZ], fields[QX]]


def minus(first, second):
    return [a - b for a, b in zip(first, second)]


def plus(first, second):
    return [a + b for a, b in zip(first, second)]


def kernel(
    n, scale, st_hbm, fw_hbm, vc_hbm, sc_hbm, cell_hbm, df_hbm, sid_hbm, out_ref, sums_ref, factor_ref,
    st, fw, vc_ref, sc_ref, cell_ref, df_ref, sid_ref, flat, tab, wide, keep, up, down, low, high, sums,
    st_sem, fw_sem, small_sem, up_sem, down_sem, sum_send, sum_recv, here,
):
    _, cells, depth = st.shape
    events = up.shape[1]
    rows = cells // events
    sources = df_ref.shape[0]
    me = lax.axis_index("gx")
    barrier = pltpu.get_barrier_semaphore()

    def greet(semaphore, peer):
        pl.semaphore_signal(semaphore, inc=1, device_id={"gx": peer}, device_id_type=pl.DeviceIdType.MESH)

    @pl.when(me > 0)
    def _():
        greet(barrier, me - 1)

    @pl.when(me < n - 1)
    def _():
        greet(barrier, me + 1)

    smalls = [
        pltpu.make_async_copy(src, dst, small_sem.at[i])
        for i, (src, dst) in enumerate(
            [(df_hbm, df_ref), (cell_hbm, cell_ref), (sid_hbm, sid_ref), (vc_hbm, vc_ref), (sc_hbm, sc_ref)]
        )
    ]
    for small in smalls:
        small.start()
    last = rows - 1
    from_hbm, to_vmem = st_hbm.reshape(8, events, rows, depth), st.reshape(8, events, rows, depth)
    loads = [
        pltpu.make_async_copy(from_hbm.at[:, :, at], to_vmem.at[:, :, at], st_sem.at[i])
        for i, at in enumerate([pl.ds(0, 2), pl.ds(last - 1, 2), pl.ds(2, rows - 4)])
    ]
    loads[0].start()
    loads[1].start()
    fw_load = pltpu.make_async_copy(fw_hbm, fw, fw_sem)
    lax.fori_loop(me + 2, n, lambda peer, _: greet(barrier, peer), None)

    @pl.when(me == 0)
    def _():
        low[...] = jnp.zeros(low.shape, jnp.float32)

    @pl.when(me == n - 1)
    def _():
        high[...] = jnp.zeros(high.shape, jnp.float32)

    for small in smalls:
        small.wait()
    vel = coeff_rows(vc_ref[...])
    coeffs = coeff_rows(sc_ref[...])

    def three(values):
        first = values.astype(jnp.bfloat16)
        rest = values - first.astype(jnp.float32)
        second = rest.astype(jnp.bfloat16)
        return [first, second, (rest - second.astype(jnp.float32)).astype(jnp.bfloat16)]

    force = jnp.concatenate([df_ref[:, t, c, :] for t in range(2) for c in range(2)], axis=0)
    count = force.shape[0]
    place = cell_ref[...] - me * (rows * depth)
    column = lax.broadcasted_iota(jnp.int32, (depth, place.shape[1]), 0)
    spot = (column // LAYER) * depth + (depth - LAYER) + lax.rem(column, LAYER)
    hot = jnp.where(spot == place, 1.0, 0.0).astype(jnp.bfloat16)
    got = lax.dot_general(
        jnp.concatenate(three(force), axis=0), hot, (((1,), (1,)), ((), ())), preferred_element_type=jnp.float32
    )
    got = got[:count] + got[count : 2 * count] + got[2 * count :]

    def placed(values, x):
        at = lax.broadcasted_iota(jnp.int32, values.shape, 1)
        return jnp.where(at < depth - LAYER, 0.0, pltpu.roll(values, depth - LAYER - x * LAYER, 1))

    row_id = lax.broadcasted_iota(jnp.int32, (8, sources), 0)
    source_at = lax.broadcasted_iota(jnp.int32, (8, sources), 1)
    blocks = []
    for b in range(events // 8):
        wanted = jnp.full((8, sources), sid_ref[b * 8], jnp.int32)
        for r in range(1, 8):
            wanted = jnp.where(row_id == r, sid_ref[b * 8 + r], wanted)
        blocks.append(jnp.where(wanted == source_at, 1.0, 0.0))
    picked = jnp.concatenate(blocks, axis=0).astype(jnp.bfloat16)
    picked = jnp.concatenate([picked] * 3, axis=1)

    def event_forcing(t):
        return [
            jnp.dot(
                picked, jnp.concatenate(three(got[(t * 2 + c) * sources : (t * 2 + c + 1) * sources]), axis=0),
                preferred_element_type=jnp.float32,
            )
            for c in range(2)
        ]

    slot_of = {0: 0, 1: 8, last: 16, last - 1: 24}
    now, later = event_forcing(0), event_forcing(1)
    force_0, force_1, force_last = [[placed(v, x) for v in now] for x in (0, 1, last)]
    later_0 = [placed(v, 0) for v in later]

    lane = lax.broadcasted_iota(jnp.int32, (8, depth), 1)
    at_row = lax.broadcasted_iota(jnp.int32, (rows, depth), 0)
    zero = jnp.zeros((8, depth), jnp.float32)
    blocks = range(events // 8)

    ups, downs = [], []
    for c in range(2):
        half = pl.ds(3 * c, 3)
        ups.append(
            pltpu.make_async_remote_copy(
                up.at[half], low.at[half], up_sem.at[0, c], up_sem.at[1, c],
                device_id={"gx": jnp.minimum(me + 1, n - 1)}, device_id_type=pl.DeviceIdType.MESH,
            )
        )
    for c, part in enumerate([pl.ds(0, 3), pl.ds(3, 1), pl.ds(4, 2)]):
        downs.append(
            pltpu.make_async_remote_copy(
                down.at[part], high.at[part], down_sem.at[0, c], down_sem.at[1, c],
                device_id={"gx": jnp.maximum(me - 1, 0)}, device_id_type=pl.DeviceIdType.MESH,
            )
        )

    def own_block(b):
        return slice(b * 8, (b + 1) * 8)

    def row(b, x, names=range(8)):
        return [st[f, pl.ds(b * 8 * rows + x, 8, stride=rows), :] for f in names]

    loads[0].wait()
    loads[2].start()
    fw_load.start()
    firsts = []
    for b in blocks:
        row_0 = row(b, 0)
        one_0 = velocity(row_0, edge(row_0), vel, lane, [v[own_block(b)] for v in force_0])
        for i, v in enumerate(front(one_0)):
            down[i, own_block(b), :] = v
        firsts.append(one_0)
    pl.semaphore_wait(barrier, me + jnp.where(me < n - 1, 1, 0))
    pl.when(me > 0)(downs[0].start)
    loads[1].wait()
    for b in blocks:
        for i, v in enumerate(row(b, last, (XX, XZ, PR))):
            up[i, own_block(b), :] = v
    pl.when(me < n - 1)(ups[0].start)
    for b in blocks:
        mine = own_block(b)
        row_0, row_1, one_0 = row(b, 0, (XX, XZ, PR)), row(b, 1), firsts[b]
        one_1 = velocity(row_1, minus(edge(row_1), row_0), vel, lane, [v[mine] for v in force_1])
        two_0 = stress(one_0, minus(front(one_1), front(one_0)), coeffs, lane)
        two_0 = velocity(two_0, edge(two_0), vel, lane, [v[mine] for v in later_0])
        down[3, mine, :] = coeffs[2] * two_0[VX] + coeffs[3] * two_0[QX]
        down[4, mine, :] = two_0[VX]
        down[5, mine, :] = two_0[VZ]
    pl.when(me > 0)(downs[1].start)
    for b in blocks:
        mine = own_block(b)
        row_last = row(b, last)
        sides = minus(edge(row_last), row(b, last - 1, (XX, XZ, PR)))
        one_last = velocity(row_last, sides, vel, lane, [v[mine] for v in force_last])
        one_last = stress(one_last, [-v for v in front(one_last)], coeffs, lane)
        for i, v in enumerate(edge(one_last)):
            up[3 + i, mine, :] = v
    pl.when(me < n - 1)(ups[1].start)

    for x in range(rows):
        flat[pl.ds(x, count, stride=rows), :] = placed(got, x)
    tab[...] = flat[...].reshape(tab.shape)
    loads[2].wait()
    fw_load.wait()
    factor_ref[0:1, :] = vel[2] * vel[3] * scale
    factor_ref[1:2, :] = coeffs[3] * scale

    def lower(values):
        return values - jnp.where(at_row == 0, 0.0, pltpu.roll(values, 1, 0))

    def upper(values):
        return jnp.where(at_row == last, 0.0, pltpu.roll(values, last, 0)) - values

    def pair(i, totals):
        perm, poro = totals
        both = pl.ds(pl.multiple_of(i * 2 * rows, 2 * rows), 2 * rows)
        stored = [fw[k, both, :].astype(jnp.float32) for k in range(6)]
        for k in range(6):
            wide[k, both, :] = stored[k]
        for half in range(2):
            e = i * 2 + half
            at = pl.ds(pl.multiple_of(e * rows, rows), rows)
            own = slice(half * rows, (half + 1) * rows)
            source = sid_ref[e]
            fields = [st[f, at, :] for f in range(8)]
            for t in range(2):
                forcing = [tab[(t * 2 + c) * sources + source] for c in range(2)]
                fields = velocity(fields, [lower(v) for v in edge(fields)], vel, lane, forcing)
                perm = perm + fields[QX] * stored[3 * t][own] + fields[QZ] * stored[3 * t + 1][own]
                fields = stress(fields, [upper(v) for v in front(fields)], coeffs, lane)
                poro = poro + fields[PR] * stored[3 * t + 2][own]
            for f in range(8):
                out_ref[f, at, :] = fields[f]
        return perm, poro

    perm, poro = lax.fori_loop(0, events // 2, pair, (zero, zero), unroll=8)

    pl.when(me > 0)(downs[2].start)
    lax.fori_loop(0, me, lambda peer, _: greet(here, peer), None)
    has_low = jnp.where(me > 0, 1.0, 0.0)
    has_high = jnp.where(me < n - 1, 1.0, 0.0)

    def seen(b, k, x):
        return wide[k, pl.ds(b * 8 * rows + x, 8, stride=rows), :]

    def add(b, x, names, values):
        for f, v in zip(names, values):
            keep[slot_of[x] + f, own_block(b), :] = v

    def sides_of(pulled):
        return [pulled[0], pulled[2], pulled[3]]

    def top(b, pulled, beyond, totals):
        perm, poro = totals
        moved = velocity_stress(pulled, vel, lane)
        perm = perm + moved[QX] * seen(b, 3, last) + moved[QZ] * seen(b, 4, last)
        prior = side_share(front(moved), coeffs)
        change = plus(pulled, stress_share(moved, minus(beyond, front(moved)), coeffs, lane))
        poro = poro + pulled[3] * seen(b, 2, last) + change[3] * seen(b, 5, last) + prior[3] * seen(b, 5, last - 1)
        return moved + change, prior, (perm, poro)

    pl.when(me > 0)(ups[0].wait_recv)
    for b in blocks:
        mine = own_block(b)
        one = velocity_share([low[i, mine, :] for i in range(3)], vel)
        perm = perm + one[QX] * seen(b, 0, 0) + one[QZ] * seen(b, 1, 0)
        met = plus([down[i, mine, :] for i in range(3)], front(one))
        rim = [v * has_low for v in beyond_share(met, coeffs)]
        two = one + stress_share(one, [-v for v in front(one)], coeffs, lane)
        poro = poro + two[PR] * seen(b, 2, 0)
        next_one = velocity_share(edge(two), vel)
        perm = perm + next_one[QX] * seen(b, 3, 1) + next_one[QZ] * seen(b, 4, 1)
        next_stress = stress_share(next_one, [-v for v in front(next_one)], coeffs, lane)
        poro = poro + next_stress[3] * seen(b, 5, 1)
        add(b, 1, range(8), next_one + next_stress)
        two = velocity(two, minus(edge(two), rim), vel, lane)
        add(b, 0, range(8), two)

        one = velocity_share([up[i, mine, :] for i in range(3)], vel)
        pulled = [v * has_high for v in side_share(front(one), coeffs)]
        two = one + stress_share(one, [-v for v in front(one)], coeffs, lane)
        full = plus([up[3 + i, mine, :] for i in range(3)], sides_of(pulled))
        beyond = [v * has_high for v in front(velocity(two, minus(edge(two), full), vel, lane))]
        own, prior, (perm, poro) = top(b, pulled, beyond, (perm, poro))
        add(b, last, range(8), own)
        add(b, last - 1, range(XX, 8), prior)

    pl.when(me < n - 1)(downs[0].wait_recv)
    for b in blocks:
        pulled = side_share([high[i, own_block(b), :] for i in range(3)], coeffs)
        beyond = front(velocity_share(sides_of(pulled), vel))
        own, prior, (perm, poro) = top(b, pulled, beyond, (perm, poro))
        add(b, last, range(8), plus(own, [keep[slot_of[last] + f, own_block(b), :] for f in range(8)]))
        more = [keep[slot_of[last - 1] + f, own_block(b), :] for f in range(XX, 8)]
        add(b, last - 1, range(XX, 8), plus(prior, more))

    pl.when(me > 0)(ups[1].wait_recv)
    for b in blocks:
        mine = own_block(b)
        late = velocity_share([low[3 + i, mine, :] for i in range(3)], vel)
        two = [keep[slot_of[0] + f, mine, :] for f in range(8)]
        two = plus(two[:4], late) + two[4:]
        perm = perm + two[QX] * seen(b, 3, 0) + two[QZ] * seen(b, 4, 0)
        after = [keep[slot_of[1] + f, mine, :] for f in (VX, VZ, QX)]
        two = stress(two, minus(after, front(two)), coeffs, lane)
        poro = poro + two[PR] * seen(b, 5, 0)
        add(b, 0, range(8), two)

    pl.when(me < n - 1)(downs[1].wait_recv)
    for b in blocks:
        poro = poro - high[3, own_block(b), :] * seen(b, 5, last)

    totals = (perm, poro)
    sums[me] = jnp.concatenate([jnp.sum(total, axis=0, keepdims=True) for total in totals], axis=0)

    @pl.when(me < n - 1)
    def _():
        pl.semaphore_wait(here, n - 1 - me)

    def send(peer, _):
        @pl.when(peer != me)
        def _():
            pltpu.make_async_remote_copy(
                sums.at[me], sums.at[me], sum_send, sum_recv,
                device_id={"gx": peer}, device_id_type=pl.DeviceIdType.MESH,
            ).start()

    lax.fori_loop(0, n, send, None)
    pl.when(me < n - 1)(downs[2].wait_recv)
    for b in blocks:
        mine = own_block(b)
        beyond_x, beyond_z = high[4, mine, :], high[5, mine, :]
        beyond_flow = (high[3, mine, :] - coeffs[2] * beyond_x) / coeffs[3]
        late = side_share([beyond_x, beyond_z, beyond_flow], coeffs)[:3] + [-high[3, mine, :]]
        add(b, last, range(XX, 8), plus([keep[slot_of[last] + f, mine, :] for f in range(XX, 8)], late))
    for b in blocks:
        for x in (0, 1, last, last - 1):
            at = pl.ds(b * 8 * rows + x, 8, stride=rows)
            for f in range(XX if x == last - 1 else 0, 8):
                out_ref[f, at, :] = out_ref[f, at, :] + keep[slot_of[x] + f, b * 8 : (b + 1) * 8, :]
    pltpu.make_async_copy(sums.at[pl.ds(1, n - 1)], sums.at[pl.ds(0, n - 1)], sum_recv).wait()
    sums_ref[...] = sums[...]
    pltpu.make_async_copy(sums.at[pl.ds(1, n - 1)], sums.at[pl.ds(0, n - 1)], sum_send).wait()
    for copy in ups:
        pl.when(me < n - 1)(copy.wait_send)
    for copy in downs:
        pl.when(me > 0)(copy.wait_send)


def write(out_ref, sums_ref, factor_ref, out_hbm, grad_hbm, grad, sems):
    half = out_ref.shape[0] // 2
    parts = [pl.ds(0, half), pl.ds(half, half)]
    copies = [pltpu.make_async_copy(out_ref.at[at], out_hbm.at[at], sems.at[i]) for i, at in enumerate(parts)]
    for copy in copies:
        copy.start()
    grad[...] = factor_ref[...] * jnp.sum(sums_ref[...], axis=0)
    copies.append(pltpu.make_async_copy(grad, grad_hbm, sems.at[2]))
    copies[2].start()
    for copy in copies:
        copy.wait()


def shards(adjoint_state, forward_fields, vel_coeffs, stress_coeffs, drm_cells, drm_force, source_id):
    fields, events, rows, depth = adjoint_state.shape
    cells = events * rows
    n = lax.axis_size("gx")
    scale = (events * rows * n) ** (-0.5)
    hbm, vmem = pl.BlockSpec(memory_space=pltpu.HBM), pl.BlockSpec(memory_space=pltpu.VMEM)
    f32 = jnp.float32
    dma = pltpu.SemaphoreType.DMA
    out, sums, factor = pl.pallas_call(
        functools.partial(kernel, n, scale),
        out_shape=[
            pltpu.VMEM((fields, cells, depth), f32),
            pltpu.VMEM((n, 2, depth), f32),
            pltpu.VMEM((2, depth), f32),
        ],
        in_specs=[hbm] * 7,
        out_specs=[vmem] * 3,
        scratch_shapes=[
            pltpu.VMEM((fields, cells, depth), f32),
            pltpu.VMEM((6, cells, depth), jnp.bfloat16),
            pltpu.VMEM(vel_coeffs.shape, f32),
            pltpu.VMEM(stress_coeffs.shape, f32),
            pltpu.VMEM((1, drm_cells.shape[0]), jnp.int32),
            pltpu.VMEM(drm_force.shape, f32),
            pltpu.SMEM(source_id.shape, jnp.int32),
            pltpu.VMEM((4 * drm_force.shape[0] * rows, depth), f32),
            pltpu.VMEM((4 * drm_force.shape[0], rows, depth), f32),
            pltpu.VMEM((6, cells, depth), f32),
            pltpu.VMEM((32, events, depth), f32),
            pltpu.VMEM((6, events, depth), f32),
            pltpu.VMEM((6, events, depth), f32),
            pltpu.VMEM((6, events, depth), f32),
            pltpu.VMEM((6, events, depth), f32),
            pltpu.VMEM((n, 2, depth), f32),
            dma((3,)),
            dma,
            dma((5,)),
            dma((2, 2)),
            dma((2, 3)),
            dma,
            dma,
            pltpu.SemaphoreType.REGULAR,
        ],
        compiler_params=pltpu.CompilerParams(
            collective_id=0, has_side_effects=True
        ),
    )(
        adjoint_state.reshape(fields, cells, depth),
        forward_fields.reshape(6, cells, depth),
        vel_coeffs,
        stress_coeffs,
        drm_cells.reshape(1, -1),
        drm_force,
        source_id,
    )
    held = [pltpu.with_memory_space_constraint(v, pltpu.VMEM) for v in (out, sums, factor)]
    out, gradients = pl.pallas_call(
        write,
        out_shape=[jax.ShapeDtypeStruct(out.shape, f32), jax.ShapeDtypeStruct(vel_coeffs[:2].shape, f32)],
        in_specs=[pl.BlockSpec(memory_space=pl.ANY), vmem, vmem],
        out_specs=[hbm, hbm],
        scratch_shapes=[pltpu.VMEM((2, depth), f32), dma((3,))],
    )(*held)
    return out.reshape(adjoint_state.shape), gradients


def solution(mesh):
    in_specs = (
        P(None, "groups", "gx", None),
        P(None, None, "groups", "gx", None),
        P("groups", None),
        P("groups", None),
        P("gx"),
        P("groups", None, None, "gx"),
        P("groups"),
    )
    out_specs = (P(None, "groups", "gx", None), P("groups", None))
    return jax.shard_map(shards, mesh=mesh, in_specs=in_specs, out_specs=out_specs, check_vma=False)
```
